256 devices in a mesh: gx: 32 (over x, z), gy: 8 (over y, core).
Axes of the slice: x: 4, y: 4, z: 8, core: 2. Of those that a mesh axis runs over, the one named last changes fastest.
Arguments:
- right_side: float32 [128, 32, 64, 256], P('gx', 'gy'), may hold values from -6 to 6
- diffusivity: float32 [128, 32, 256], P('gx', 'gy'), may hold values from 1 to 4
- agglomerate: int32 [128, 32, 256], P('gx', 'gy'), may hold values from 0 to 31, as said below
- element_matrix: float32 [64, 64], replicated, may hold values from -0.3 to 4.3, as said below
- face_matrices: float32 [6, 64, 64], replicated, may hold values from -0.375 to 0.375
- restriction: float32 [64], replicated, may hold values from 0.008 to 0.024
- prolongation: float32 [64], replicated, may hold values from 0.5 to 1.5
- coarse_shift: float32 [32, 8, 32], P('gx', 'gy'), may hold values from 0.05 to 0.5
Outputs:
- solution: float32 [128, 32, 64, 256], P('gx', 'gy')
- coarse_correction: float32 [32, 8, 32], P('gx', 'gy')
The draws below stay inside these ranges and needn't reach their ends.
Inputs may be any that keep to these rules, and one draw needn't show every extreme that they name: `agglomerate`: in every column of 256 elements the values never fall along z and each value from 0 to 31 occurs. `element_matrix`: entries lie within 3.7 to 4.3 on the diagonal and within -0.3 to 0.3 off it.
All inputs are finite; a program needn't handle non-finite values.
Results may differ from the reference program's by a relative error of at most 0.0003.
Values sent between devices are 32-bit elements; how exact they have to be, the bound alone decides.
A program may use at most 64 MiB of HBM per device.

```python
import math
import jax
import jax.numpy as jnp
from jax import lax

NP = 64
CX = 4
CY = 4
EZ = 256
KC = 32
ITC = 24
EX = 128
EY = 32
GRID_X = 32
GRID_Y = 8
N_GX = 32
N_GY = 8


def draw_right_side(key, part):
    key = jax.random.fold_in(key, 11)
    shape = (EX, EY, NP, EZ)
    return jnp.clip(jax.random.normal(key, shape, jnp.float32), -6.0, 6.0)


def draw_element_matrix(key, part):
    key = jax.random.fold_in(key, 23)
    spread = jax.random.uniform(key, (NP, NP), jnp.float32, -0.3, 0.3)
    row_index = jnp.arange(NP, dtype=jnp.int32)[:, None]
    col_index = jnp.arange(NP, dtype=jnp.int32)[None, :]
    return spread + 4.0 * (row_index == col_index).astype(jnp.float32)


def draw_agglomerate(key, part):
    key = jax.random.fold_in(key, 37)
    scores = jax.random.randint(key, (EX, EY, EZ - 1), 0, 1 << 16, dtype=jnp.int32) * EZ
    scores = scores + jnp.arange(EZ - 1, dtype=jnp.int32)
    unused, picked = lax.top_k(scores, KC - 1)
    x_index = jnp.arange(EX, dtype=jnp.int32)[:, None, None]
    y_index = jnp.arange(EY, dtype=jnp.int32)[None, :, None]
    starts = jnp.zeros((EX, EY, EZ), jnp.int32).at[x_index, y_index, picked + 1].set(1)
    return jnp.cumsum(starts, axis=2).astype(jnp.int32)


def block_scale(key, dims, cuts, least, top_value):
    factor_of, own = 1.0, jax.random.fold_in(key, 6)
    for axis_at, parts in cuts:
        draws = jnp.exp(jax.random.uniform(jax.random.fold_in(own, axis_at), (parts,), jnp.float32, least / len(cuts), top_value / len(cuts)))
        factor_of = factor_of * jnp.repeat(draws, dims[axis_at] // parts).reshape([-1 if axis == axis_at else 1 for axis in range(len(dims))])
    return factor_of


def scatter_about(stream_key, dims, width, limit, kind=jnp.bfloat16):
    entries = jax.random.normal(stream_key, dims, jnp.float32) * width
    return jnp.minimum(jnp.maximum(entries, -limit), limit).astype(kind)


def setup_inputs(seed: int = 0) -> dict:
    seeds = jax.random.split(jax.random.key(seed), 9)
    right_side = draw_right_side(jax.random.fold_in(seeds[8], 71), 0)
    diffusivity = jnp.clip(jnp.exp(math.log(4.0) - 1.3862944 * jax.random.uniform(seeds[1], (EX, EY, EZ), jnp.float32) ** block_scale(seeds[1], (EX, EY, EZ), ((0, 32), (1, 8)), -0.2, 0.2)), 1.0, 4.0)
    agglomerate = draw_agglomerate(jax.random.fold_in(seeds[8], 71), 0)
    element_matrix = draw_element_matrix(jax.random.fold_in(seeds[8], 71), 0)
    face_matrices = scatter_about(seeds[4], (6, NP, NP), 256 ** -0.5, 0.375, jnp.float32)
    restriction = jnp.clip(jax.random.uniform(seeds[5], (NP,), jnp.float32, 0.008, 0.024), 0.008, 0.024)
    prolongation = jnp.clip(jax.random.uniform(seeds[6], (NP,), jnp.float32, 0.5, 1.5), 0.5, 1.5)
    coarse_shift = jnp.clip(jnp.exp(math.log(0.5) - 2.3025851 * jax.random.uniform(seeds[7], (GRID_X, GRID_Y, KC), jnp.float32) ** block_scale(seeds[7], (GRID_X, GRID_Y, KC), ((0, 32), (1, 8)), -0.2, 0.2)), 0.05, 0.5)
    return {"right_side": right_side, "diffusivity": diffusivity, "agglomerate": agglomerate, "element_matrix": element_matrix, "face_matrices": face_matrices, "restriction": restriction, "prolongation": prolongation, "coarse_shift": coarse_shift}


damping = 0.8


def couple(values, face_matrices):
    highest = lax.Precision.HIGHEST
    padded = jnp.pad(values, ((1, 1), (1, 1), (0, 0), (1, 1)))
    pieces = (padded[:-2, 1:-1, :, 1:-1], padded[2:, 1:-1, :, 1:-1], padded[1:-1, :-2, :, 1:-1], padded[1:-1, 2:, :, 1:-1], padded[1:-1, 1:-1, :, :-2], padded[1:-1, 1:-1, :, 2:])
    summed = jnp.zeros_like(values)
    for direction in range(6):
        summed = summed + jnp.einsum('ij,xyjz->xyiz', face_matrices[direction], pieces[direction], precision=highest)
    return summed


def operate(values, element_matrix, face_matrices):
    own_term = jnp.einsum('ij,xyjz->xyiz', element_matrix, values, precision=lax.Precision.HIGHEST)
    return own_term - couple(values, face_matrices)


def reference(right_side, diffusivity, agglomerate, element_matrix, face_matrices, restriction, prolongation, coarse_shift):
    highest = lax.Precision.HIGHEST
    diagonal = jnp.diagonal(element_matrix)[None, None, :, None]
    weight = diffusivity[:, :, None, :]
    source = right_side / weight
    solution = jnp.zeros_like(right_side)
    for repeat in range(2):
        solution = solution + damping * (source - operate(solution, element_matrix, face_matrices)) / diagonal
    residual = right_side - weight * operate(solution, element_matrix, face_matrices)
    reduced = jnp.einsum('i,xyiz->xyz', restriction, residual, precision=highest)
    blocks = reduced.reshape(N_GX, CX, N_GY, CY, EZ)
    labels = agglomerate.reshape(N_GX, CX, N_GY, CY, EZ)
    onehot = (labels[..., None] == jnp.arange(KC, dtype=jnp.int32)).astype(jnp.float32)
    coarse_rhs = jnp.einsum('aibjz,aibjzk->abk', blocks, onehot, precision=highest)
    pivots = 6.0 + coarse_shift
    correction = jnp.zeros_like(coarse_rhs)
    for repeat in range(ITC):
        padded = jnp.pad(correction, 1)
        beside_all = padded[:-2, 1:-1, 1:-1] + padded[2:, 1:-1, 1:-1] + padded[1:-1, :-2, 1:-1]
        beside_all = beside_all + padded[1:-1, 2:, 1:-1] + padded[1:-1, 1:-1, :-2] + padded[1:-1, 1:-1, 2:]
        correction = (coarse_rhs + beside_all) / pivots
    lifted = jnp.einsum('abk,aibjzk->aibjz', correction, onehot, precision=highest).reshape(EX, EY, EZ)
    solution = solution + prolongation[None, None, :, None] * lifted[:, :, None, :]
    solution = solution + damping * (source - operate(solution, element_matrix, face_matrices)) / diagonal
    return solution, correction
```

```python
import functools

import jax
import jax.numpy as jnp
from jax import lax
from jax.experimental import pallas as pl
from jax.experimental.pallas import tpu as pltpu
from jax.sharding import PartitionSpec as P

NP = 64
EZ = 256
KC = 32
ITC = 24
SIDE = 4
COLS = SIDE * SIDE
PADS = SIDE + 2
damping = 0.8
highest = lax.Precision.HIGHEST
MESH = pl.DeviceIdType.MESH
f32, bf16 = jnp.float32, jnp.bfloat16


def halves(values):
    high = values.astype(bf16)
    return high, (values - high.astype(f32)).astype(bf16)


def iota(shape, axis):
    return lax.broadcasted_iota(jnp.int32, shape, axis)


def after(rows):
    return jnp.where(iota(rows.shape, 1) == 0, 0.0, pltpu.roll(rows, 1, 1))


def before(rows):
    last = rows.shape[1] - 1
    return jnp.where(iota(rows.shape, 1) == last, 0.0, pltpu.roll(rows, last, 1))


SOURCE = (
    lambda c: (SIDE - 1) * SIDE + c,
    lambda c: c,
    lambda c: c * SIDE + SIDE - 1,
    lambda c: c * SIDE,
)


def padded_slot(side, c):
    return (c + 1, (PADS - 1) * PADS + c + 1, (c + 1) * PADS, (c + 1) * PADS + PADS - 1)[side]


def exchange_kernel(
    gxn, gyn, zn,
    rhs_hbm, w_ref, agg_ref, e_ref, f_ref, r_ref, p_ref, shift_ref,
    base_ref, coef_ref, grhs_ref, gpiv_ref, aggh_ref,
    rhs_v, u1, u2, hal1, hal2, p1h, p1l, p2h, p2l, own_w, side_w,
    trow, tsend, thalo, asend, ahalo,
    s1a, r1a, s2a, r2a, s1b, r1b, s2b, r2b,
    load_sem, send1, recv1, send2, recv2, tsend_sem, trecv_sem, asend_sem, arecv_sem,
    gsem_a, gsem_b,
):
    gx, gy = lax.axis_index("gx"), lax.axis_index("gy")
    xg, zg = gx // zn, gx % zn
    xn = gxn // zn
    group = xn * gyn
    mine = xg * gyn + gy
    has = (gx > 0, gx < gxn - 1, gy > 0, gy < gyn - 1)
    sends = (has[1], has[0], has[3], has[2])
    target = ((gx + 1, gy), (gx - 1, gy), (gx, gy + 1), (gx, gy - 1))

    barrier = pltpu.get_barrier_semaphore()
    for s in (0, 1):
        @pl.when(sends[s])
        def _(s=s):
            pl.semaphore_signal(barrier, inc=1, device_id=target[s], device_id_type=MESH)

    def greet_plane(j, carry):
        @pl.when(j != mine)
        def _():
            pl.semaphore_signal(
                barrier, inc=1, device_id=((j // gyn) * zn + zg, j % gyn), device_id_type=MESH)
        return carry

    lax.fori_loop(0, group, greet_plane, 0)

    def greet_line(j, carry):
        @pl.when(j != zg)
        def _():
            pl.semaphore_signal(
                barrier, inc=1, device_id=(xg * zn + j, gy), device_id_type=MESH)
        return carry

    lax.fori_loop(0, zn, greet_line, 0)

    def load(x):
        return pltpu.make_async_copy(
            rhs_hbm.at[x], rhs_v.at[pl.ds(x * SIDE, SIDE)], load_sem.at[x])

    for x in (0, 3, 1, 2):
        load(x).start()

    same = iota((NP, NP), 0) == iota((NP, NP), 1)
    element = e_ref[...]
    on_diagonal = jnp.where(same, element, 0.0)
    diagonal = jnp.sum(on_diagonal, axis=1, keepdims=True)
    scale = damping / diagonal
    r_row = r_ref[...].reshape(1, NP)
    p_row = p_ref[...].reshape(1, NP)
    r_col = jnp.sum(jnp.where(same, r_row, 0.0), axis=1, keepdims=True)
    p_col = jnp.sum(jnp.where(same, p_row, 0.0), axis=1, keepdims=True)
    faces = [f_ref[d] for d in range(6)]
    scaled = [scale * face for face in faces]
    own_scaled = scale * element
    rows = [jnp.sum(r_col * m, axis=0, keepdims=True) for m in [element] + faces]
    rows.append(r_row * jnp.sum(on_diagonal, axis=0, keepdims=True) / damping)
    stacked = jnp.concatenate(
        [own_scaled, scaled[4], scaled[5]] + rows + [jnp.zeros((8, NP), f32)], axis=0)
    high, low = halves(stacked)
    own_w[:, 0:64] = high
    own_w[:, 64:128] = high
    own_w[:, 128:192] = low
    own_w[:, 192:256] = low
    for d in range(4):
        high, low = halves(scaled[d])
        side_w[0:64, d * 64:d * 64 + 64] = high
        side_w[64:128, d * 64:d * 64 + 64] = low

    for x in (0, 3, 1, 2):
        load(x).wait()

        def first(y, carry, x=x):
            col = x * SIDE + y
            value = rhs_v[col] * (1.0 / w_ref[x, pl.ds(y, 1), :]) * scale
            u1[col] = value
            slot = (x + 1) * PADS + y + 1
            p1h[slot], p1l[slot] = halves(value)
            return carry

        lax.fori_loop(0, SIDE, first, 0)

    asend[0] = agg_ref[SIDE - 1]
    asend[1] = agg_ref[0]
    for c in range(SIDE):
        asend[2, c:c + 1, :] = agg_ref[c, SIDE - 1:SIDE, :]
        asend[3, c:c + 1, :] = agg_ref[c, 0:1, :]

    in_group = iota((1, 128), 1) // KC == xg

    def spread(row):
        return jnp.where(in_group, jnp.concatenate([row] * 4, axis=1), 0.0)

    expected = group - 1 + zn - 1 + has[0].astype(jnp.int32) + has[1].astype(jnp.int32)
    pl.semaphore_wait(barrier, expected)

    def face(values, halo, send, recv, s, c):
        return pltpu.make_async_remote_copy(
            src_ref=values.at[SOURCE[s](c)], dst_ref=halo.at[s, c],
            send_sem=send.at[s, c], recv_sem=recv.at[s, c],
            device_id=target[s], device_id_type=MESH)

    face1 = functools.partial(face, u1, hal1, send1, recv1)
    face2 = functools.partial(face, u2, hal2, send2, recv2)

    def start(make, s, c):
        @pl.when(sends[s])
        def _():
            make(s, c).start()

    for c in range(SIDE):
        for s in range(4):
            start(face1, s, c)

    def small(values, halo, send, recv, s):
        return pltpu.make_async_remote_copy(
            src_ref=values.at[s], dst_ref=halo.at[s], send_sem=send.at[s], recv_sem=recv.at[s],
            device_id=target[s], device_id_type=MESH)

    labels = functools.partial(small, asend, ahalo, asend_sem, arecv_sem)
    scalars = functools.partial(small, tsend, thalo, tsend_sem, trecv_sem)

    for s in range(4):
        @pl.when(sends[s])
        def _(s=s):
            labels(s).start()

    def gather_first(s1, r1, sems, row):
        s1[...] = row
        r1[mine] = row

        def step(j, carry):
            @pl.when(j != mine)
            def _():
                pltpu.make_async_remote_copy(
                    src_ref=s1, dst_ref=r1.at[mine], send_sem=sems.at[0], recv_sem=sems.at[1],
                    device_id=((j // gyn) * zn + zg, j % gyn), device_id_type=MESH).start()
            return carry

        lax.fori_loop(0, group, step, 0)

    def wait_bytes(ref, count, sem):
        part = ref.at[pl.ds(0, count)]
        pltpu.make_async_copy(part, part, sem).wait()

    def gather_second(r1, s2, r2, sems):
        wait_bytes(r1, group - 1, sems.at[1])
        if gyn < 8:
            s2[...] = jnp.zeros_like(s2)
        for b in range(gyn):
            s2[b:b + 1, :] = sum(r1[q * gyn + b] for q in range(xn))
        r2[zg] = s2[...]

        def step(j, carry):
            @pl.when(j != zg)
            def _():
                pltpu.make_async_remote_copy(
                    src_ref=s2, dst_ref=r2.at[zg], send_sem=sems.at[2], recv_sem=sems.at[3],
                    device_id=(xg * zn + j, gy), device_id_type=MESH).start()
            return carry

        lax.fori_loop(0, zn, step, 0)

    def gather_third(r1, r2, sems, out):
        wait_bytes(r2, zn - 1, sems.at[3])
        out[...] = r2[...]
        wait_bytes(r1, group - 1, sems.at[0])
        wait_bytes(r2, zn - 1, sems.at[2])

    gather_first(s1a, r1a, gsem_a, spread(1.0 / (6.0 + shift_ref[0])))

    nothing = jnp.zeros((NP, EZ), bf16)
    for s in range(4):
        @pl.when(jnp.logical_not(has[s]))
        def _(s=s):
            thalo[s] = jnp.zeros((SIDE, EZ), f32)
            ahalo[s] = jnp.zeros((SIDE, EZ), jnp.int32)
            for c in range(SIDE):
                slot = padded_slot(s, c)
                p1h[slot] = nothing
                p1l[slot] = nothing
                p2h[slot] = nothing
                p2l[slot] = nothing

    own_matrix = own_w
    side_matrix = side_w

    def own_part(high_ref, low_ref, slot):
        high, low = high_ref[slot], low_ref[slot]
        g = jnp.dot(own_matrix[...], jnp.concatenate([high, low, high, low], axis=0),
                    preferred_element_type=f32)
        return g[0:64] - after(g[64:128]) - before(g[128:192]), g[192:200]

    def side_part(high_ref, low_ref, slot):
        around = (slot - PADS, slot + PADS, slot - 1, slot + 1)
        high = jnp.concatenate([high_ref[s] for s in around], axis=0)
        low = jnp.concatenate([low_ref[s] for s in around], axis=0)
        both = jnp.dot(side_matrix[...], high, preferred_element_type=f32)
        return both[0:64] + both[64:128] + jnp.dot(
            side_matrix[0:64, :], low, preferred_element_type=f32)

    def second(x, y):
        col, slot = x * SIDE + y, (x + 1) * PADS + y + 1
        before_it = u1[col]
        own, from_u1 = own_part(p1h, p1l, slot)
        value = 2.0 * before_it - own + side_part(p1h, p1l, slot)
        u2[col] = value
        p2h[slot], p2l[slot] = halves(value)
        own, from_u2 = own_part(p2h, p2l, slot)
        base_ref[col] = value + before_it - own
        total = from_u1[7:8] - from_u2[0:1] + after(from_u2[5:6]) + before(from_u2[6:7])
        trow[col] = jnp.where(iota((8, EZ), 0) == 0, total, from_u2)

    def arrive(make, halo, high_ref, low_ref, s, c):
        @pl.when(has[s])
        def _():
            make(s, c).wait_recv()
            slot = padded_slot(s, c)
            high_ref[slot], low_ref[slot] = halves(halo[s, c])

    arrive1 = functools.partial(arrive, face1, hal1, p1h, p1l)
    arrive2 = functools.partial(arrive, face2, hal2, p2h, p2l)

    def interior(i, carry):
        second(1, i + 1)
        second(2, i + 1)
        return carry

    lax.fori_loop(0, 2, interior, 0)
    for c in range(SIDE):
        for s in (2, 3):
            arrive1(s, c)
    gather_second(r1a, s2a, r2a, gsem_a)

    def side_y(i, carry):
        second(i + 1, 0)
        second(i + 1, SIDE - 1)
        return carry

    lax.fori_loop(0, 2, side_y, 0)
    for c in (1, 2):
        for s in (2, 3):
            start(face2, s, c)
    for c in range(SIDE):
        arrive1(0, c)
        arrive1(1, c)
        second(0, c)
        second(SIDE - 1, c)
        start(face2, 0, c)
        start(face2, 1, c)
        if c in (0, SIDE - 1):
            s = 3 if c == 0 else 2
            start(face2, s, 0)
            start(face2, s, SIDE - 1)

    for s in range(4):
        for c in range(SIDE):
            tsend[s, c:c + 1, :] = trow[SOURCE[s](c), s + 1:s + 2, :]

        @pl.when(sends[s])
        def _(s=s):
            scalars(s).start()

    def last(x, y):
        col, slot = x * SIDE + y, (x + 1) * PADS + y + 1
        base_ref[col] += side_part(p2h, p2l, slot)

    def last_interior(i, carry):
        last(1, i + 1)
        last(2, i + 1)
        return carry

    lax.fori_loop(0, 2, last_interior, 0)

    for s in range(4):
        @pl.when(has[s])
        def _(s=s):
            scalars(s).wait_recv()

    levels = iota((KC, EZ), 0)
    total = jnp.zeros((KC, EZ), f32)
    for x in range(SIDE):
        for y in range(SIDE):
            col = x * SIDE + y
            row = trow[col, 0:1, :]
            row += trow[col - SIDE, 1:2, :] if x > 0 else thalo[0, y:y + 1, :]
            row += trow[col + SIDE, 2:3, :] if x < SIDE - 1 else thalo[1, y:y + 1, :]
            row += trow[col - 1, 3:4, :] if y > 0 else thalo[2, x:x + 1, :]
            row += trow[col + 1, 4:5, :] if y < SIDE - 1 else thalo[3, x:x + 1, :]
            row = row * w_ref[x, y:y + 1, :]
            total += jnp.where(agg_ref[x, y:y + 1, :] == levels, row, 0.0)
    sums = lax.dot_general(
        jnp.ones((8, EZ), f32), jnp.concatenate([total] * 4, axis=0),
        (((1,), (1,)), ((), ())), precision=highest, preferred_element_type=f32)
    gather_first(s1b, r1b, gsem_b, jnp.where(in_group, sums[0:1], 0.0))

    for c in range(SIDE):
        for s in (2, 3):
            arrive2(s, c)

    def last_y(i, carry):
        last(i + 1, 0)
        last(i + 1, SIDE - 1)
        return carry

    lax.fori_loop(0, 2, last_y, 0)
    gather_second(r1b, s2b, r2b, gsem_b)

    gains = [jnp.sum(m * p_row, axis=1, keepdims=True) for m in scaled]
    own_gain = p_col - jnp.sum(own_scaled * p_row, axis=1, keepdims=True)
    lane = iota((NP, 256), 1)
    at = lane % 64

    def coefficients(col, carry):
        x, y = col // SIDE, col % SIDE
        places = (
            jnp.where(x > 0, col - SIDE, COLS + y),
            jnp.where(x < SIDE - 1, col + SIDE, COLS + SIDE + y),
            jnp.where(y > 0, col - 1, COLS + 2 * SIDE + x),
            jnp.where(y < SIDE - 1, col + 1, COLS + 3 * SIDE + x),
            2 * COLS + col,
            3 * COLS + col,
        )
        matrix = jnp.where(at == col, own_gain, 0.0)
        for d in range(6):
            matrix = jnp.where(at == places[d], gains[d], matrix)
        high, low = halves(matrix)
        coef_ref[col] = jnp.where(lane < 128, high.astype(f32), low.astype(f32)).astype(bf16)
        return carry

    lax.fori_loop(0, COLS, coefficients, 0)

    for c in range(SIDE):
        arrive2(0, c)
        arrive2(1, c)
        last(0, c)
        last(SIDE - 1, c)

    for s in range(4):
        @pl.when(has[s])
        def _(s=s):
            labels(s).wait_recv()
    aggh_ref[...] = ahalo[...]
    gather_third(r1a, r2a, gsem_a, gpiv_ref)
    gather_third(r1b, r2b, gsem_b, grhs_ref)

    for s in range(4):
        @pl.when(sends[s])
        def _(s=s):
            labels(s).wait_send()
            scalars(s).wait_send()
            for c in range(SIDE):
                face1(s, c).wait_send()
                face2(s, c).wait_send()


def finish_kernel(
    gxn, gyn, zn,
    base_ref, coef_ref, grhs_ref, gpiv_ref, aggh_ref, agg_ref,
    out_hbm, corr_ref,
    out_v, coarse, labels, lifted, out_sem,
):
    gx, gy = lax.axis_index("gx"), lax.axis_index("gy")
    lane, sub = iota((8, 128), 1), iota((8, 128), 0)
    level = lane % KC

    rhs = [grhs_ref[i] for i in range(zn)]
    pivot = [gpiv_ref[i] for i in range(zn)]

    def sweep(repeat, now):
        new = []
        wrap_low = jnp.where(lane < KC, 0.0, pltpu.roll(now[zn - 1], KC, 1))
        wrap_high = jnp.where(lane >= 128 - KC, 0.0, pltpu.roll(now[0], 128 - KC, 1))
        for i in range(zn):
            value = now[i]
            total = rhs[i] + (now[i - 1] if i > 0 else wrap_low)
            total += now[i + 1] if i < zn - 1 else wrap_high
            total += jnp.where(sub == 0, 0.0, pltpu.roll(value, 1, 0))
            total += jnp.where(sub == 7, 0.0, pltpu.roll(value, 7, 0))
            total += jnp.where(level == 0, 0.0, pltpu.roll(value, 1, 1))
            total += jnp.where(level == KC - 1, 0.0, pltpu.roll(value, 127, 1))
            new.append(total * pivot[i])
        return tuple(new)

    now = lax.fori_loop(0, ITC - 1, sweep, tuple(a * b for a, b in zip(rhs, pivot)))
    for i in range(zn):
        coarse[i] = now[i]

    def table(ax, ay):
        shifted = ax + zn
        value = coarse[shifted % zn]
        value = jnp.where((sub == ay) & (lane // KC == shifted // zn - 1), value, 0.0)
        row = jnp.sum(value, axis=0, keepdims=True)
        row = row + pltpu.roll(row, 64, 1)
        return row + pltpu.roll(row, 32, 1)

    own = table(gx, gy)
    corr_ref[0] = own[:, :KC]
    sides = [table(gx - 1, gy), table(gx + 1, gy), table(gx, gy - 1), table(gx, gy + 1)]
    tables = [jnp.broadcast_to(own, (8, 128))] * 2 + [
        jnp.where(sub < 4, sides[0], sides[1]), jnp.where(sub < 4, sides[2], sides[3])]
    for x in range(SIDE):
        labels[x * SIDE:(x + 1) * SIDE, :] = agg_ref[x]
        labels[COLS + x * SIDE:COLS + (x + 1) * SIDE, :] = aggh_ref[x]
    for i in range(4):
        for half in range(2):
            picked = labels[i * 8:i * 8 + 8, half * 128:half * 128 + 128]
            lifted[i * 8:i * 8 + 8, half * 128:half * 128 + 128] = jnp.take_along_axis(
                tables[i], picked, axis=1)
    lifted[32:48, :] = after(lifted[0:16, :])
    lifted[48:64, :] = before(lifted[0:16, :])
    high, low = halves(lifted[...])
    around = jnp.concatenate([high, low, high, low], axis=0)

    def store(x):
        return pltpu.make_async_copy(
            out_v.at[pl.ds(x * SIDE, SIDE)], out_hbm.at[x], out_sem.at[x])

    for x in range(SIDE):
        for y in range(SIDE):
            col = x * SIDE + y
            out_v[col] = base_ref[col] + jnp.dot(coef_ref[col], around, preferred_element_type=f32)
        store(x).start()
    for x in range(SIDE):
        store(x).wait()


def body(gxn, gyn, zn, right_side, diffusivity, agglomerate, element_matrix, face_matrices,
         restriction, prolongation, coarse_shift):
    group = gxn // zn * gyn
    vmem = pl.BlockSpec(memory_space=pltpu.VMEM)
    hbm = pl.BlockSpec(memory_space=pl.ANY)
    dma = pltpu.SemaphoreType.DMA
    field = pltpu.VMEM((COLS, NP, EZ), f32)
    halo = pltpu.VMEM((4, SIDE, NP, EZ), f32)
    parts = pltpu.VMEM((PADS * PADS, NP, EZ), bf16)
    gather = [
        pltpu.VMEM((1, 128), f32),
        pltpu.VMEM((group, 1, 128), f32),
        pltpu.VMEM((8, 128), f32),
        pltpu.VMEM((zn, 8, 128), f32),
    ]
    side_rows = pltpu.VMEM((4, SIDE, EZ), f32)
    side_labels = pltpu.VMEM((4, SIDE, EZ), jnp.int32)
    base, coef, grhs, gpiv, aggh = pl.pallas_call(
        functools.partial(exchange_kernel, gxn, gyn, zn),
        out_shape=(
            jax.ShapeDtypeStruct((COLS, NP, EZ), f32),
            jax.ShapeDtypeStruct((COLS, NP, 256), bf16),
            jax.ShapeDtypeStruct((zn, 8, 128), f32),
            jax.ShapeDtypeStruct((zn, 8, 128), f32),
            jax.ShapeDtypeStruct((4, SIDE, EZ), jnp.int32),
        ),
        in_specs=[hbm] + [vmem] * 7,
        out_specs=(vmem,) * 5,
        scratch_shapes=[
            field, field, field, halo, halo, parts, parts, parts, parts,
            pltpu.VMEM((208, 256), bf16), pltpu.VMEM((128, 256), bf16),
            pltpu.VMEM((COLS, 8, EZ), f32), side_rows, side_rows, side_labels, side_labels,
            *gather, *gather,
            dma((SIDE,)), dma((4, SIDE)), dma((4, SIDE)), dma((4, SIDE)), dma((4, SIDE)),
            dma((4,)), dma((4,)), dma((4,)), dma((4,)), dma((4,)), dma((4,)),
        ],
        compiler_params=pltpu.CompilerParams(
            collective_id=0, has_side_effects=True, vmem_limit_bytes=40 * 2**20),
        name="exchange",
    )(right_side, diffusivity, agglomerate, element_matrix, face_matrices, restriction,
      prolongation, coarse_shift)
    return pl.pallas_call(
        functools.partial(finish_kernel, gxn, gyn, zn),
        out_shape=(
            jax.ShapeDtypeStruct((SIDE, SIDE, NP, EZ), f32),
            jax.ShapeDtypeStruct((1, 1, KC), f32),
        ),
        in_specs=[vmem] * 6,
        out_specs=(hbm, vmem),
        scratch_shapes=[
            field, pltpu.VMEM((zn, 8, 128), f32), pltpu.VMEM((32, EZ), jnp.int32),
            pltpu.VMEM((64, EZ), f32), dma((SIDE,)),
        ],
        compiler_params=pltpu.CompilerParams(vmem_limit_bytes=20 * 2**20),
        name="finish",
    )(base, coef, grhs, gpiv, aggh, agglomerate)


def solution(mesh):
    gxn, gyn = mesh.shape["gx"], mesh.shape["gy"]
    return jax.shard_map(
        functools.partial(body, gxn, gyn, max(1, gxn // 4)),
        mesh=mesh,
        in_specs=(
            P("gx", "gy", None, None),
            P("gx", "gy", None),
            P("gx", "gy", None),
            P(),
            P(),
            P(),
            P(),
            P("gx", "gy", None),
        ),
        out_specs=(P("gx", "gy", None, None), P("gx", "gy", None)),
        check_vma=False,
    )
```

```python
import functools

import jax
import jax.numpy as jnp
from jax import lax
from jax.experimental import pallas as pl
from jax.experimental.pallas import tpu as pltpu
from jax.sharding import PartitionSpec as P

NP = 64
EZ = 256
KC = 32
ITC = 24
SIDE = 4
COLS = SIDE * SIDE
PADS = SIDE + 2
damping = 0.8
highest = lax.Precision.HIGHEST
MESH = pl.DeviceIdType.MESH
f32, bf16 = jnp.float32, jnp.bfloat16


def halves(values):
    high = values.astype(bf16)
    return high, (values - high.astype(f32)).astype(bf16)


def iota(shape, axis):
    return lax.broadcasted_iota(jnp.int32, shape, axis)


def after(rows):
    return jnp.where(iota(rows.shape, 1) == 0, 0.0, pltpu.roll(rows, 1, 1))


def before(rows):
    last = rows.shape[1] - 1
    return jnp.where(iota(rows.shape, 1) == last, 0.0, pltpu.roll(rows, last, 1))


SOURCE = (
    lambda c: (SIDE - 1) * SIDE + c,
    lambda c: c,
    lambda c: c * SIDE + SIDE - 1,
    lambda c: c * SIDE,
)


def padded_slot(side, c):
    return (c + 1, (PADS - 1) * PADS + c + 1, (c + 1) * PADS, (c + 1) * PADS + PADS - 1)[side]


def exchange_kernel(
    gxn, gyn, zn,
    rhs_hbm, w_hbm, agg_hbm, e_hbm, f_hbm, r_hbm, p_hbm, shift_hbm,
    base_ref, coef_ref, grhs_ref, gpiv_ref, labels_ref,
    w_ref, agg_ref, e_ref, f_ref, r_ref, p_ref, shift_ref, rhs_v, u1, u2, hal1, hal2, p1h, p1l, p2h, p2l, own_w, side_w,
    trow, tsend, thalo, asend, ahalo,
    s1a, r1a, s2a, r2a, s1b, r1b, s2b, r2b,
    small_sem, load_sem, send1, recv1, send2, recv2, tsend_sem, trecv_sem, asend_sem, arecv_sem,
    gsem_a, gsem_b,
):
    gx, gy = lax.axis_index("gx"), lax.axis_index("gy")
    xg, zg = gx // zn, gx % zn
    xn = gxn // zn
    group = xn * gyn
    mine = xg * gyn + gy
    has = (gx > 0, gx < gxn - 1, gy > 0, gy < gyn - 1)
    sends = (has[1], has[0], has[3], has[2])
    target = ((gx + 1, gy), (gx - 1, gy), (gx, gy + 1), (gx, gy - 1))

    def load(x):
        return pltpu.make_async_copy(
            rhs_hbm.at[x], rhs_v.at[pl.ds(x * SIDE, SIDE)], load_sem.at[x])

    inputs = [
        pltpu.make_async_copy(a, b, small_sem.at[i]) for i, (a, b) in enumerate((
            (e_hbm, e_ref), (f_hbm, f_ref), (r_hbm, r_ref), (p_hbm, p_ref), (w_hbm, w_ref),
            (shift_hbm, shift_ref), (agg_hbm, agg_ref)))]
    for copy in inputs:
        copy.start()
    for x in (0, 3, 1, 2):
        load(x).start()

    barrier = pltpu.get_barrier_semaphore()
    for s in (0, 1):
        @pl.when(sends[s])
        def _(s=s):
            pl.semaphore_signal(barrier, inc=1, device_id=target[s], device_id_type=MESH)

    def greet_plane(j, carry):
        @pl.when(j != mine)
        def _():
            pl.semaphore_signal(
                barrier, inc=1, device_id=((j // gyn) * zn + zg, j % gyn), device_id_type=MESH)
        return carry

    lax.fori_loop(0, group, greet_plane, 0)

    def greet_line(j, carry):
        @pl.when(j != zg)
        def _():
            pl.semaphore_signal(
                barrier, inc=1, device_id=(xg * zn + j, gy), device_id_type=MESH)
        return carry

    lax.fori_loop(0, zn, greet_line, 0)

    for copy in inputs:
        copy.wait()

    same = iota((NP, NP), 0) == iota((NP, NP), 1)
    element = e_ref[...]
    on_diagonal = jnp.where(same, element, 0.0)
    diagonal = jnp.sum(on_diagonal, axis=1, keepdims=True)
    scale = damping / diagonal
    r_row = r_ref[...].reshape(1, NP)
    p_row = p_ref[...].reshape(1, NP)
    r_col = jnp.sum(jnp.where(same, r_row, 0.0), axis=1, keepdims=True)
    p_col = jnp.sum(jnp.where(same, p_row, 0.0), axis=1, keepdims=True)
    faces = [f_ref[d] for d in range(6)]
    scaled = [scale * face for face in faces]
    own_scaled = scale * element
    rows = [jnp.sum(r_col * m, axis=0, keepdims=True) for m in [element] + faces]
    rows.append(r_row * jnp.sum(on_diagonal, axis=0, keepdims=True) / damping)
    stacked = jnp.concatenate(
        [own_scaled, scaled[4], scaled[5]] + rows + [jnp.zeros((8, NP), f32)], axis=0)
    high, low = halves(stacked)
    own_w[:, 0:64] = high
    own_w[:, 64:128] = high
    own_w[:, 128:192] = low
    own_w[:, 192:256] = low
    for d in range(4):
        high, low = halves(scaled[d])
        side_w[0:64, d * 64:d * 64 + 64] = high
        side_w[64:128, d * 64:d * 64 + 64] = low

    for x in (0, 3, 1, 2):
        load(x).wait()

        def first(y, carry, x=x):
            col = x * SIDE + y
            value = rhs_v[col] * (1.0 / w_ref[x, pl.ds(y, 1), :]) * scale
            u1[col] = value
            slot = (x + 1) * PADS + y + 1
            p1h[slot], p1l[slot] = halves(value)
            return carry

        lax.fori_loop(0, SIDE, first, 0)

    for x in range(SIDE):
        labels_ref[x * SIDE:(x + 1) * SIDE, :] = agg_ref[x]
    asend[0] = agg_ref[SIDE - 1]
    asend[1] = agg_ref[0]
    for c in range(SIDE):
        asend[2, c:c + 1, :] = agg_ref[c, SIDE - 1:SIDE, :]
        asend[3, c:c + 1, :] = agg_ref[c, 0:1, :]

    in_group = iota((1, 128), 1) // KC == xg

    def spread(row):
        return jnp.where(in_group, jnp.concatenate([row] * 4, axis=1), 0.0)

    expected = group - 1 + zn - 1 + has[0].astype(jnp.int32) + has[1].astype(jnp.int32)
    pl.semaphore_wait(barrier, expected)

    def face(values, halo, send, recv, s, c):
        return pltpu.make_async_remote_copy(
            src_ref=values.at[SOURCE[s](c)], dst_ref=halo.at[s, c],
            send_sem=send.at[s, c], recv_sem=recv.at[s, c],
            device_id=target[s], device_id_type=MESH)

    face1 = functools.partial(face, u1, hal1, send1, recv1)
    face2 = functools.partial(face, u2, hal2, send2, recv2)

    def start(make, s, c):
        @pl.when(sends[s])
        def _():
            make(s, c).start()

    for c in range(SIDE):
        for s in range(4):
            start(face1, s, c)

    def small(values, halo, send, recv, s):
        return pltpu.make_async_remote_copy(
            src_ref=values.at[s], dst_ref=halo.at[s], send_sem=send.at[s], recv_sem=recv.at[s],
            device_id=target[s], device_id_type=MESH)

    labels = functools.partial(small, asend, ahalo, asend_sem, arecv_sem)
    scalars = functools.partial(small, tsend, thalo, tsend_sem, trecv_sem)

    for s in range(4):
        @pl.when(sends[s])
        def _(s=s):
            labels(s).start()

    def gather_first(s1, r1, sems, row):
        s1[...] = row
        r1[mine] = row

        def step(j, carry):
            @pl.when(j != mine)
            def _():
                pltpu.make_async_remote_copy(
                    src_ref=s1, dst_ref=r1.at[mine], send_sem=sems.at[0], recv_sem=sems.at[1],
                    device_id=((j // gyn) * zn + zg, j % gyn), device_id_type=MESH).start()
            return carry

        lax.fori_loop(0, group, step, 0)

    def wait_bytes(ref, count, sem):
        part = ref.at[pl.ds(0, count)]
        pltpu.make_async_copy(part, part, sem).wait()

    def gather_second(r1, s2, r2, sems):
        wait_bytes(r1, group - 1, sems.at[1])
        if gyn < 8:
            s2[...] = jnp.zeros_like(s2)
        for b in range(gyn):
            s2[b:b + 1, :] = sum(r1[q * gyn + b] for q in range(xn))
        r2[zg] = s2[...]

        def step(j, carry):
            @pl.when(j != zg)
            def _():
                pltpu.make_async_remote_copy(
                    src_ref=s2, dst_ref=r2.at[zg], send_sem=sems.at[2], recv_sem=sems.at[3],
                    device_id=(xg * zn + j, gy), device_id_type=MESH).start()
            return carry

        lax.fori_loop(0, zn, step, 0)

    def gather_third(r1, r2, sems, out):
        wait_bytes(r2, zn - 1, sems.at[3])
        out[...] = r2[...]
        wait_bytes(r1, group - 1, sems.at[0])
        wait_bytes(r2, zn - 1, sems.at[2])

    gather_first(s1a, r1a, gsem_a, spread(1.0 / (6.0 + shift_ref[0])))

    nothing = jnp.zeros((NP, EZ), bf16)
    for s in range(4):
        @pl.when(jnp.logical_not(has[s]))
        def _(s=s):
            thalo[s] = jnp.zeros((SIDE, EZ), f32)
            ahalo[s] = jnp.zeros((SIDE, EZ), jnp.int32)
            for c in range(SIDE):
                slot = padded_slot(s, c)
                p1h[slot] = nothing
                p1l[slot] = nothing
                p2h[slot] = nothing
                p2l[slot] = nothing

    own_matrix = own_w
    side_matrix = side_w

    def own_part(high_ref, low_ref, slot):
        high, low = high_ref[slot], low_ref[slot]
        g = jnp.dot(own_matrix[...], jnp.concatenate([high, low, high, low], axis=0),
                    preferred_element_type=f32)
        return g[0:64] - after(g[64:128]) - before(g[128:192]), g[192:200]

    def side_part(high_ref, low_ref, slot):
        around = (slot - PADS, slot + PADS, slot - 1, slot + 1)
        high = jnp.concatenate([high_ref[s] for s in around], axis=0)
        low = jnp.concatenate([low_ref[s] for s in around], axis=0)
        both = jnp.dot(side_matrix[...], high, preferred_element_type=f32)
        return both[0:64] + both[64:128] + jnp.dot(
            side_matrix[0:64, :], low, preferred_element_type=f32)

    def second(x, y):
        col, slot = x * SIDE + y, (x + 1) * PADS + y + 1
        before_it = u1[col]
        own, from_u1 = own_part(p1h, p1l, slot)
        value = 2.0 * before_it - own + side_part(p1h, p1l, slot)
        u2[col] = value
        p2h[slot], p2l[slot] = halves(value)
        own, from_u2 = own_part(p2h, p2l, slot)
        base_ref[col] = value + before_it - own
        total = from_u1[7:8] - from_u2[0:1] + after(from_u2[5:6]) + before(from_u2[6:7])
        trow[col] = jnp.where(iota((8, EZ), 0) == 0, total, from_u2)

    def arrive(make, halo, high_ref, low_ref, s, c):
        @pl.when(has[s])
        def _():
            make(s, c).wait_recv()
            slot = padded_slot(s, c)
            high_ref[slot], low_ref[slot] = halves(halo[s, c])

    arrive1 = functools.partial(arrive, face1, hal1, p1h, p1l)
    arrive2 = functools.partial(arrive, face2, hal2, p2h, p2l)

    def interior(i, carry):
        second(1, i + 1)
        second(2, i + 1)
        return carry

    lax.fori_loop(0, 2, interior, 0)
    for c in range(SIDE):
        for s in (2, 3):
            arrive1(s, c)
    gather_second(r1a, s2a, r2a, gsem_a)

    def side_y(i, carry):
        second(i + 1, 0)
        second(i + 1, SIDE - 1)
        return carry

    lax.fori_loop(0, 2, side_y, 0)
    for c in (1, 2):
        for s in (2, 3):
            start(face2, s, c)
    for c in range(SIDE):
        arrive1(0, c)
        arrive1(1, c)
        second(0, c)
        second(SIDE - 1, c)
        start(face2, 0, c)
        start(face2, 1, c)
        if c in (0, SIDE - 1):
            s = 3 if c == 0 else 2
            start(face2, s, 0)
            start(face2, s, SIDE - 1)

    for s in range(4):
        for c in range(SIDE):
            tsend[s, c:c + 1, :] = trow[SOURCE[s](c), s + 1:s + 2, :]

        @pl.when(sends[s])
        def _(s=s):
            scalars(s).start()

    def last(x, y):
        col, slot = x * SIDE + y, (x + 1) * PADS + y + 1
        base_ref[col] += side_part(p2h, p2l, slot)

    def last_interior(i, carry):
        last(1, i + 1)
        last(2, i + 1)
        return carry

    lax.fori_loop(0, 2, last_interior, 0)

    for s in range(4):
        @pl.when(has[s])
        def _(s=s):
            scalars(s).wait_recv()

    levels = iota((KC, EZ), 0)
    total = jnp.zeros((KC, EZ), f32)
    for x in range(SIDE):
        for y in range(SIDE):
            col = x * SIDE + y
            row = trow[col, 0:1, :]
            row += trow[col - SIDE, 1:2, :] if x > 0 else thalo[0, y:y + 1, :]
            row += trow[col + SIDE, 2:3, :] if x < SIDE - 1 else thalo[1, y:y + 1, :]
            row += trow[col - 1, 3:4, :] if y > 0 else thalo[2, x:x + 1, :]
            row += trow[col + 1, 4:5, :] if y < SIDE - 1 else thalo[3, x:x + 1, :]
            row = row * w_ref[x, y:y + 1, :]
            total += jnp.where(agg_ref[x, y:y + 1, :] == levels, row, 0.0)
    sums = lax.dot_general(
        jnp.ones((8, EZ), f32), jnp.concatenate([total] * 4, axis=0),
        (((1,), (1,)), ((), ())), precision=highest, preferred_element_type=f32)
    gather_first(s1b, r1b, gsem_b, jnp.where(in_group, sums[0:1], 0.0))

    for c in range(SIDE):
        for s in (2, 3):
            arrive2(s, c)

    def last_y(i, carry):
        last(i + 1, 0)
        last(i + 1, SIDE - 1)
        return carry

    lax.fori_loop(0, 2, last_y, 0)
    gather_second(r1b, s2b, r2b, gsem_b)

    gains = [jnp.sum(m * p_row, axis=1, keepdims=True) for m in scaled]
    own_gain = p_col - jnp.sum(own_scaled * p_row, axis=1, keepdims=True)
    lane = iota((NP, 256), 1)
    at = lane % 64

    def coefficients(col, carry):
        x, y = col // SIDE, col % SIDE
        places = (
            jnp.where(x > 0, col - SIDE, COLS + y),
            jnp.where(x < SIDE - 1, col + SIDE, COLS + SIDE + y),
            jnp.where(y > 0, col - 1, COLS + 2 * SIDE + x),
            jnp.where(y < SIDE - 1, col + 1, COLS + 3 * SIDE + x),
            2 * COLS + col,
            3 * COLS + col,
        )
        matrix = jnp.where(at == col, own_gain, 0.0)
        for d in range(6):
            matrix = jnp.where(at == places[d], gains[d], matrix)
        high, low = halves(matrix)
        coef_ref[col] = jnp.where(lane < 128, high.astype(f32), low.astype(f32)).astype(bf16)
        return carry

    lax.fori_loop(0, COLS, coefficients, 0)

    for c in range(SIDE):
        arrive2(0, c)
        arrive2(1, c)
        last(0, c)
        last(SIDE - 1, c)

    for s in range(4):
        @pl.when(has[s])
        def _(s=s):
            labels(s).wait_recv()
    for s in range(4):
        labels_ref[COLS + s * SIDE:COLS + (s + 1) * SIDE, :] = ahalo[s]
    gather_third(r1a, r2a, gsem_a, gpiv_ref)
    gather_third(r1b, r2b, gsem_b, grhs_ref)

    for s in range(4):
        @pl.when(sends[s])
        def _(s=s):
            labels(s).wait_send()
            scalars(s).wait_send()
            for c in range(SIDE):
                face1(s, c).wait_send()
                face2(s, c).wait_send()


def finish_kernel(
    gxn, gyn, zn,
    base_ref, coef_ref, grhs_ref, gpiv_ref, labels,
    out_hbm, corr_ref,
    out_v, coarse, lifted, out_sem,
):
    gx, gy = lax.axis_index("gx"), lax.axis_index("gy")
    lane, sub = iota((8, 128), 1), iota((8, 128), 0)
    level = lane % KC

    rhs = [grhs_ref[i] for i in range(zn)]
    pivot = [gpiv_ref[i] for i in range(zn)]

    def sweep(repeat, now):
        new = []
        wrap_low = jnp.where(lane < KC, 0.0, pltpu.roll(now[zn - 1], KC, 1))
        wrap_high = jnp.where(lane >= 128 - KC, 0.0, pltpu.roll(now[0], 128 - KC, 1))
        for i in range(zn):
            value = now[i]
            total = rhs[i] + (now[i - 1] if i > 0 else wrap_low)
            total += now[i + 1] if i < zn - 1 else wrap_high
            total += jnp.where(sub == 0, 0.0, pltpu.roll(value, 1, 0))
            total += jnp.where(sub == 7, 0.0, pltpu.roll(value, 7, 0))
            total += jnp.where(level == 0, 0.0, pltpu.roll(value, 1, 1))
            total += jnp.where(level == KC - 1, 0.0, pltpu.roll(value, 127, 1))
            new.append(total * pivot[i])
        return tuple(new)

    now = lax.fori_loop(0, ITC - 1, sweep, tuple(a * b for a, b in zip(rhs, pivot)))
    for i in range(zn):
        coarse[i] = now[i]

    def table(ax, ay):
        shifted = ax + zn
        value = coarse[shifted % zn]
        value = jnp.where((sub == ay) & (lane // KC == shifted // zn - 1), value, 0.0)
        row = jnp.sum(value, axis=0, keepdims=True)
        row = row + pltpu.roll(row, 64, 1)
        return row + pltpu.roll(row, 32, 1)

    own = table(gx, gy)
    corr_ref[0] = own[:, :KC]
    sides = [table(gx - 1, gy), table(gx + 1, gy), table(gx, gy - 1), table(gx, gy + 1)]
    tables = [jnp.broadcast_to(own, (8, 128))] * 2 + [
        jnp.where(sub < 4, sides[0], sides[1]), jnp.where(sub < 4, sides[2], sides[3])]
    for i in range(4):
        for half in range(2):
            picked = labels[i * 8:i * 8 + 8, half * 128:half * 128 + 128]
            lifted[i * 8:i * 8 + 8, half * 128:half * 128 + 128] = jnp.take_along_axis(
                tables[i], picked, axis=1)
    lifted[32:48, :] = after(lifted[0:16, :])
    lifted[48:64, :] = before(lifted[0:16, :])
    high, low = halves(lifted[...])
    around = jnp.concatenate([high, low, high, low], axis=0)

    def store(x):
        return pltpu.make_async_copy(
            out_v.at[pl.ds(x * SIDE, SIDE)], out_hbm.at[x], out_sem.at[x])

    for x in range(SIDE):
        for y in range(SIDE):
            col = x * SIDE + y
            out_v[col] = base_ref[col] + jnp.dot(coef_ref[col], around, preferred_element_type=f32)
        store(x).start()
    for x in range(SIDE):
        store(x).wait()


def body(gxn, gyn, zn, right_side, diffusivity, agglomerate, element_matrix, face_matrices,
         restriction, prolongation, coarse_shift):
    group = gxn // zn * gyn
    vmem = pl.BlockSpec(memory_space=pltpu.VMEM)
    hbm = pl.BlockSpec(memory_space=pl.ANY)
    dma = pltpu.SemaphoreType.DMA
    field = pltpu.VMEM((COLS, NP, EZ), f32)
    halo = pltpu.VMEM((4, SIDE, NP, EZ), f32)
    parts = pltpu.VMEM((PADS * PADS, NP, EZ), bf16)
    gather = [
        pltpu.VMEM((1, 128), f32),
        pltpu.VMEM((group, 1, 128), f32),
        pltpu.VMEM((8, 128), f32),
        pltpu.VMEM((zn, 8, 128), f32),
    ]
    side_rows = pltpu.VMEM((4, SIDE, EZ), f32)
    side_labels = pltpu.VMEM((4, SIDE, EZ), jnp.int32)
    base, coef, grhs, gpiv, labels = pl.pallas_call(
        functools.partial(exchange_kernel, gxn, gyn, zn),
        out_shape=(
            jax.ShapeDtypeStruct((COLS, NP, EZ), f32),
            jax.ShapeDtypeStruct((COLS, NP, 256), bf16),
            jax.ShapeDtypeStruct((zn, 8, 128), f32),
            jax.ShapeDtypeStruct((zn, 8, 128), f32),
            jax.ShapeDtypeStruct((2 * COLS, EZ), jnp.int32),
        ),
        in_specs=[pl.BlockSpec(memory_space=pltpu.HBM)] * 8,
        out_specs=(vmem,) * 5,
        scratch_shapes=[
            pltpu.VMEM((SIDE, SIDE, EZ), f32), pltpu.VMEM((SIDE, SIDE, EZ), jnp.int32),
            pltpu.VMEM((NP, NP), f32), pltpu.VMEM((6, NP, NP), f32), pltpu.VMEM((NP,), f32),
            pltpu.VMEM((NP,), f32), pltpu.VMEM((1, 1, KC), f32),
            field, field, field, halo, halo, parts, parts, parts, parts,
            pltpu.VMEM((208, 256), bf16), pltpu.VMEM((128, 256), bf16),
            pltpu.VMEM((COLS, 8, EZ), f32), side_rows, side_rows, side_labels, side_labels,
            *gather, *gather,
            dma((7,)), dma((SIDE,)), dma((4, SIDE)), dma((4, SIDE)), dma((4, SIDE)), dma((4, SIDE)),
            dma((4,)), dma((4,)), dma((4,)), dma((4,)), dma((4,)), dma((4,)),
        ],
        compiler_params=pltpu.CompilerParams(
            collective_id=0, has_side_effects=True, vmem_limit_bytes=40 * 2**20),
        name="exchange",
    )(*[pltpu.with_memory_space_constraint(value, pltpu.HBM) for value in (
        right_side, diffusivity, agglomerate, element_matrix, face_matrices, restriction,
        prolongation, coarse_shift)])
    return pl.pallas_call(
        functools.partial(finish_kernel, gxn, gyn, zn),
        out_shape=(
            jax.ShapeDtypeStruct((SIDE, SIDE, NP, EZ), f32),
            jax.ShapeDtypeStruct((1, 1, KC), f32),
        ),
        in_specs=[vmem] * 5,
        out_specs=(hbm, vmem),
        scratch_shapes=[
            field, pltpu.VMEM((zn, 8, 128), f32), pltpu.VMEM((64, EZ), f32), dma((SIDE,)),
        ],
        compiler_params=pltpu.CompilerParams(vmem_limit_bytes=20 * 2**20),
        name="finish",
    )(base, coef, grhs, gpiv, labels)


def solution(mesh):
    gxn, gyn = mesh.shape["gx"], mesh.shape["gy"]
    return jax.shard_map(
        functools.partial(body, gxn, gyn, max(1, gxn // 4)),
        mesh=mesh,
        in_specs=(
            P("gx", "gy", None, None),
            P("gx", "gy", None),
            P("gx", "gy", None),
            P(),
            P(),
            P(),
            P(),
            P("gx", "gy", None),
        ),
        out_specs=(P("gx", "gy", None, None), P("gx", "gy", None)),
        check_vma=False,
    )
```

```python
import functools

import jax
import jax.numpy as jnp
from jax import lax
from jax.experimental import pallas as pl
from jax.experimental.pallas import tpu as pltpu
from jax.sharding import PartitionSpec as P

NP = 64
EZ = 256
KC = 32
ITC = 24
SIDE = 4
COLS = SIDE * SIDE
PADS = SIDE + 2
damping = 0.8
highest = lax.Precision.HIGHEST
MESH = pl.DeviceIdType.MESH
f32, bf16 = jnp.float32, jnp.bfloat16


def halves(values):
    high = values.astype(bf16)
    return high, (values - high.astype(f32)).astype(bf16)


def iota(shape, axis):
    return lax.broadcasted_iota(jnp.int32, shape, axis)


def after(rows):
    return jnp.where(iota(rows.shape, 1) == 0, 0.0, pltpu.roll(rows, 1, 1))


def before(rows):
    last = rows.shape[1] - 1
    return jnp.where(iota(rows.shape, 1) == last, 0.0, pltpu.roll(rows, last, 1))


SOURCE = (
    lambda c: (SIDE - 1) * SIDE + c,
    lambda c: c,
    lambda c: c * SIDE + SIDE - 1,
    lambda c: c * SIDE,
)


def padded_slot(side, c):
    return (c + 1, (PADS - 1) * PADS + c + 1, (c + 1) * PADS, (c + 1) * PADS + PADS - 1)[side]


def exchange_kernel(
    gxn, gyn, zn,
    rhs_hbm, w_hbm, agg_hbm, e_hbm, f_hbm, r_hbm, p_hbm, shift_hbm,
    base_ref, coef_ref, grhs_ref, gpiv_ref, labels_ref,
    w_ref, agg_ref, e_ref, f_ref, r_ref, p_ref, shift_ref, rhs_v, u1, u2, hal1, hal2, p1h, p1l, p2h, p2l, own_w, side_w, path_w,
    field, qsend, qhalo, trow, tsend, thalo, asend, ahalo,
    s1a, r1a, s2a, r2a, s1b, r1b, s2b, r2b,
    small_sem, load_sem, send1, recv1, send2, recv2, tsend_sem, trecv_sem, asend_sem, arecv_sem,
    gsem_a, gsem_b, qsend_sem, qrecv_sem,
):
    gx, gy = lax.axis_index("gx"), lax.axis_index("gy")
    xg, zg = gx // zn, gx % zn
    xn = gxn // zn
    group = xn * gyn
    mine = xg * gyn + gy
    has = (gx > 0, gx < gxn - 1, gy > 0, gy < gyn - 1)
    sends = (has[1], has[0], has[3], has[2])
    target = ((gx + 1, gy), (gx - 1, gy), (gx, gy + 1), (gx, gy - 1))

    def load(x):
        return pltpu.make_async_copy(
            rhs_hbm.at[x], rhs_v.at[pl.ds(x * SIDE, SIDE)], load_sem.at[x])

    inputs = [
        pltpu.make_async_copy(a, b, small_sem.at[i]) for i, (a, b) in enumerate((
            (e_hbm, e_ref), (f_hbm, f_ref), (r_hbm, r_ref), (p_hbm, p_ref), (w_hbm, w_ref),
            (shift_hbm, shift_ref), (agg_hbm, agg_ref)))]
    for copy in inputs:
        copy.start()
    for x in (0, 3, 1, 2):
        load(x).start()

    barrier = pltpu.get_barrier_semaphore()
    for s in (0, 1):
        @pl.when(sends[s])
        def _(s=s):
            pl.semaphore_signal(barrier, inc=1, device_id=target[s], device_id_type=MESH)

    def greet_plane(j, carry):
        @pl.when(j != mine)
        def _():
            pl.semaphore_signal(
                barrier, inc=1, device_id=((j // gyn) * zn + zg, j % gyn), device_id_type=MESH)
        return carry

    lax.fori_loop(0, group, greet_plane, 0)

    def greet_line(j, carry):
        @pl.when(j != zg)
        def _():
            pl.semaphore_signal(
                barrier, inc=1, device_id=(xg * zn + j, gy), device_id_type=MESH)
        return carry

    lax.fori_loop(0, zn, greet_line, 0)

    for copy in inputs:
        copy.wait()

    same = iota((NP, NP), 0) == iota((NP, NP), 1)
    element = e_ref[...]
    on_diagonal = jnp.where(same, element, 0.0)
    diagonal = jnp.sum(on_diagonal, axis=1, keepdims=True)
    scale = damping / diagonal
    r_row = r_ref[...].reshape(1, NP)
    p_row = p_ref[...].reshape(1, NP)
    r_col = jnp.sum(jnp.where(same, r_row, 0.0), axis=1, keepdims=True)
    p_col = jnp.sum(jnp.where(same, p_row, 0.0), axis=1, keepdims=True)
    faces = [f_ref[d] for d in range(6)]
    scaled = [scale * face for face in faces]
    own_scaled = scale * element
    rows = [jnp.sum(r_col * m, axis=0, keepdims=True) for m in [element] + faces]
    rows.append(r_row * jnp.sum(on_diagonal, axis=0, keepdims=True) / damping)

    def lay(weights, matrix):
        high, low = halves(matrix)
        weights[:, 0:64] = high
        weights[:, 64:128] = high
        weights[:, 128:192] = low
        weights[:, 192:256] = low

    lay(own_w, jnp.concatenate([own_scaled, scaled[4], scaled[5]], axis=0))

    reduce_rows = jnp.concatenate(rows[0:7] + [jnp.zeros((1, NP), f32)], axis=0)
    scaled_rows = reduce_rows * (damping / jnp.sum(on_diagonal, axis=0, keepdims=True))
    products = [jnp.dot(scaled_rows, m, precision=highest, preferred_element_type=f32)
                for m in [element] + faces]
    lay(path_w, jnp.concatenate(
        [2.0 * reduce_rows - products[0]] + products[1:] + [rows[7], jnp.zeros((7, NP), f32)], axis=0))
    for d in range(4):
        high, low = halves(scaled[d])
        side_w[0:64, d * 64:d * 64 + 64] = high
        side_w[64:128, d * 64:d * 64 + 64] = low

    for x in (0, 3, 1, 2):
        load(x).wait()

        def first(y, carry, x=x):
            col = x * SIDE + y
            value = rhs_v[col] * (1.0 / w_ref[x, pl.ds(y, 1), :]) * scale
            u1[col] = value
            slot = (x + 1) * PADS + y + 1
            p1h[slot], p1l[slot] = halves(value)
            return carry

        lax.fori_loop(0, SIDE, first, 0)

    for x in range(SIDE):
        labels_ref[x * SIDE:(x + 1) * SIDE, :] = agg_ref[x]
    asend[0] = agg_ref[SIDE - 1]
    asend[1] = agg_ref[0]
    for c in range(SIDE):
        asend[2, c:c + 1, :] = agg_ref[c, SIDE - 1:SIDE, :]
        asend[3, c:c + 1, :] = agg_ref[c, 0:1, :]

    in_group = iota((1, 128), 1) // KC == xg

    def spread(row):
        return jnp.where(in_group, jnp.concatenate([row] * 4, axis=1), 0.0)

    expected = group - 1 + zn - 1 + has[0].astype(jnp.int32) + has[1].astype(jnp.int32)
    pl.semaphore_wait(barrier, expected)

    def face(values, halo, send, recv, s, c):
        return pltpu.make_async_remote_copy(
            src_ref=values.at[SOURCE[s](c)], dst_ref=halo.at[s, c],
            send_sem=send.at[s, c], recv_sem=recv.at[s, c],
            device_id=target[s], device_id_type=MESH)

    face1 = functools.partial(face, u1, hal1, send1, recv1)
    face2 = functools.partial(face, u2, hal2, send2, recv2)

    def start(make, s, c):
        @pl.when(sends[s])
        def _():
            make(s, c).start()

    for c in range(SIDE):
        for s in range(4):
            start(face1, s, c)

    def small(values, halo, send, recv, s):
        return pltpu.make_async_remote_copy(
            src_ref=values.at[s], dst_ref=halo.at[s], send_sem=send.at[s], recv_sem=recv.at[s],
            device_id=target[s], device_id_type=MESH)

    paths = functools.partial(small, qsend, qhalo, qsend_sem, qrecv_sem)
    labels = functools.partial(small, asend, ahalo, asend_sem, arecv_sem)
    scalars = functools.partial(small, tsend, thalo, tsend_sem, trecv_sem)

    def follow(x, carry):
        for y in range(SIDE):
            col, slot = x * SIDE + y, (x + 1) * PADS + y + 1
            high, low = p1h[slot], p1l[slot]
            field[col] = jnp.dot(path_w[...], jnp.concatenate([high, low, high, low], axis=0),
                                 preferred_element_type=f32)
        return carry

    lax.fori_loop(0, SIDE, follow, 0)
    for s in range(4):
        for c in range(SIDE):
            qsend[s, c] = field[SOURCE[s](c), 8 + 8 * s:16 + 8 * s, :]

        @pl.when(sends[s])
        def _(s=s):
            paths(s).start()
            labels(s).start()

    def gather_first(s1, r1, sems, row):
        s1[...] = row
        r1[mine] = row

        def step(j, carry):
            @pl.when(j != mine)
            def _():
                pltpu.make_async_remote_copy(
                    src_ref=s1, dst_ref=r1.at[mine], send_sem=sems.at[0], recv_sem=sems.at[1],
                    device_id=((j // gyn) * zn + zg, j % gyn), device_id_type=MESH).start()
            return carry

        lax.fori_loop(0, group, step, 0)

    def wait_bytes(ref, count, sem):
        part = ref.at[pl.ds(0, count)]
        pltpu.make_async_copy(part, part, sem).wait()

    def gather_second(r1, s2, r2, sems):
        wait_bytes(r1, group - 1, sems.at[1])
        if gyn < 8:
            s2[...] = jnp.zeros_like(s2)
        for b in range(gyn):
            s2[b:b + 1, :] = sum(r1[q * gyn + b] for q in range(xn))
        r2[zg] = s2[...]

        def step(j, carry):
            @pl.when(j != zg)
            def _():
                pltpu.make_async_remote_copy(
                    src_ref=s2, dst_ref=r2.at[zg], send_sem=sems.at[2], recv_sem=sems.at[3],
                    device_id=(xg * zn + j, gy), device_id_type=MESH).start()
            return carry

        lax.fori_loop(0, zn, step, 0)

    def gather_third(r1, r2, sems, out):
        wait_bytes(r2, zn - 1, sems.at[3])
        out[...] = r2[...]
        wait_bytes(r1, group - 1, sems.at[0])
        wait_bytes(r2, zn - 1, sems.at[2])

    gather_first(s1a, r1a, gsem_a, spread(1.0 / (6.0 + shift_ref[0])))

    nothing = jnp.zeros((NP, EZ), bf16)
    for s in range(4):
        @pl.when(jnp.logical_not(has[s]))
        def _(s=s):
            thalo[s] = jnp.zeros((SIDE, EZ), f32)
            qhalo[s] = jnp.zeros((SIDE, 8, EZ), f32)
            ahalo[s] = jnp.zeros((SIDE, EZ), jnp.int32)
            for c in range(SIDE):
                slot = padded_slot(s, c)
                p1h[slot] = nothing
                p1l[slot] = nothing
                p2h[slot] = nothing
                p2l[slot] = nothing

    own_matrix = own_w
    side_matrix = side_w

    def own_part(high_ref, low_ref, slot):
        high, low = high_ref[slot], low_ref[slot]
        g = jnp.dot(own_matrix[...], jnp.concatenate([high, low, high, low], axis=0),
                    preferred_element_type=f32)
        return g[0:64] - after(g[64:128]) - before(g[128:192])

    def side_part(high_ref, low_ref, slot):
        around = (slot - PADS, slot + PADS, slot - 1, slot + 1)
        high = jnp.concatenate([high_ref[s] for s in around], axis=0)
        low = jnp.concatenate([low_ref[s] for s in around], axis=0)
        both = jnp.dot(side_matrix[...], high, preferred_element_type=f32)
        return both[0:64] + both[64:128] + jnp.dot(
            side_matrix[0:64, :], low, preferred_element_type=f32)

    def second(x, y):
        col, slot = x * SIDE + y, (x + 1) * PADS + y + 1
        before_it = u1[col]
        value = 2.0 * before_it - own_part(p1h, p1l, slot) + side_part(p1h, p1l, slot)
        u2[col] = value
        p2h[slot], p2l[slot] = halves(value)
        base_ref[col] = value + before_it - own_part(p2h, p2l, slot)

    def arrive(make, halo, high_ref, low_ref, s, c):
        @pl.when(has[s])
        def _():
            make(s, c).wait_recv()
            slot = padded_slot(s, c)
            high_ref[slot], low_ref[slot] = halves(halo[s, c])

    arrive1 = functools.partial(arrive, face1, hal1, p1h, p1l)
    arrive2 = functools.partial(arrive, face2, hal2, p2h, p2l)

    def interior(i, carry):
        second(1, i + 1)
        second(2, i + 1)
        return carry

    lax.fori_loop(0, 2, interior, 0)

    for s in range(4):
        @pl.when(has[s])
        def _(s=s):
            paths(s).wait_recv()
    for x in range(SIDE):
        for y in range(SIDE):
            col = x * SIDE + y
            value = field[col, 0:8, :] + after(field[col, 40:48, :]) + before(field[col, 48:56, :])
            value += field[col - SIDE, 8:16, :] if x > 0 else qhalo[0, y]
            value += field[col + SIDE, 16:24, :] if x < SIDE - 1 else qhalo[1, y]
            value += field[col - 1, 24:32, :] if y > 0 else qhalo[2, x]
            value += field[col + 1, 32:40, :] if y < SIDE - 1 else qhalo[3, x]
            total = field[col, 56:57, :] - value[0:1] + after(value[5:6]) + before(value[6:7])
            trow[col] = jnp.where(iota((8, EZ), 0) == 0, total, value)
    for s in range(4):
        for c in range(SIDE):
            tsend[s, c:c + 1, :] = trow[SOURCE[s](c), s + 1:s + 2, :]

        @pl.when(sends[s])
        def _(s=s):
            scalars(s).start()

    for c in range(SIDE):
        for s in (2, 3):
            arrive1(s, c)
    gather_second(r1a, s2a, r2a, gsem_a)

    def side_y(i, carry):
        second(i + 1, 0)
        second(i + 1, SIDE - 1)
        return carry

    lax.fori_loop(0, 2, side_y, 0)
    for c in (1, 2):
        for s in (2, 3):
            start(face2, s, c)

    for s in range(4):
        @pl.when(has[s])
        def _(s=s):
            scalars(s).wait_recv()

    levels = iota((KC, EZ), 0)
    total = jnp.zeros((KC, EZ), f32)
    for x in range(SIDE):
        for y in range(SIDE):
            col = x * SIDE + y
            row = trow[col, 0:1, :]
            row += trow[col - SIDE, 1:2, :] if x > 0 else thalo[0, y:y + 1, :]
            row += trow[col + SIDE, 2:3, :] if x < SIDE - 1 else thalo[1, y:y + 1, :]
            row += trow[col - 1, 3:4, :] if y > 0 else thalo[2, x:x + 1, :]
            row += trow[col + 1, 4:5, :] if y < SIDE - 1 else thalo[3, x:x + 1, :]
            row = row * w_ref[x, y:y + 1, :]
            total += jnp.where(agg_ref[x, y:y + 1, :] == levels, row, 0.0)
    sums = lax.dot_general(
        jnp.ones((8, EZ), f32), jnp.concatenate([total] * 4, axis=0),
        (((1,), (1,)), ((), ())), precision=highest, preferred_element_type=f32)
    gather_first(s1b, r1b, gsem_b, jnp.where(in_group, sums[0:1], 0.0))

    for c in range(SIDE):
        arrive1(0, c)
        arrive1(1, c)
        second(0, c)
        second(SIDE - 1, c)
        start(face2, 0, c)
        start(face2, 1, c)
        if c in (0, SIDE - 1):
            s = 3 if c == 0 else 2
            start(face2, s, 0)
            start(face2, s, SIDE - 1)

    gather_second(r1b, s2b, r2b, gsem_b)

    def last(x, y):
        col, slot = x * SIDE + y, (x + 1) * PADS + y + 1
        base_ref[col] += side_part(p2h, p2l, slot)

    def last_interior(i, carry):
        last(1, i + 1)
        last(2, i + 1)
        return carry

    lax.fori_loop(0, 2, last_interior, 0)

    for c in range(SIDE):
        for s in (2, 3):
            arrive2(s, c)

    def last_y(i, carry):
        last(i + 1, 0)
        last(i + 1, SIDE - 1)
        return carry

    lax.fori_loop(0, 2, last_y, 0)

    gains = [jnp.sum(m * p_row, axis=1, keepdims=True) for m in scaled]
    own_gain = p_col - jnp.sum(own_scaled * p_row, axis=1, keepdims=True)
    lane = iota((NP, 256), 1)
    at = lane % 64

    def coefficients(col, carry):
        x, y = col // SIDE, col % SIDE
        places = (
            jnp.where(x > 0, col - SIDE, COLS + y),
            jnp.where(x < SIDE - 1, col + SIDE, COLS + SIDE + y),
            jnp.where(y > 0, col - 1, COLS + 2 * SIDE + x),
            jnp.where(y < SIDE - 1, col + 1, COLS + 3 * SIDE + x),
            2 * COLS + col,
            3 * COLS + col,
        )
        matrix = jnp.where(at == col, own_gain, 0.0)
        for d in range(6):
            matrix = jnp.where(at == places[d], gains[d], matrix)
        high, low = halves(matrix)
        coef_ref[col] = jnp.where(lane < 128, high.astype(f32), low.astype(f32)).astype(bf16)
        return carry

    lax.fori_loop(0, COLS, coefficients, 0)

    for c in range(SIDE):
        arrive2(0, c)
        arrive2(1, c)
        last(0, c)
        last(SIDE - 1, c)

    for s in range(4):
        @pl.when(has[s])
        def _(s=s):
            labels(s).wait_recv()
    for s in range(4):
        labels_ref[COLS + s * SIDE:COLS + (s + 1) * SIDE, :] = ahalo[s]
    gather_third(r1a, r2a, gsem_a, gpiv_ref)
    gather_third(r1b, r2b, gsem_b, grhs_ref)

    for s in range(4):
        @pl.when(sends[s])
        def _(s=s):
            labels(s).wait_send()
            scalars(s).wait_send()
            paths(s).wait_send()
            for c in range(SIDE):
                face1(s, c).wait_send()
                face2(s, c).wait_send()


def finish_kernel(
    gxn, gyn, zn,
    base_ref, coef_ref, grhs_ref, gpiv_ref, labels,
    out_hbm, corr_ref,
    out_v, coarse, lifted, out_sem,
):
    gx, gy = lax.axis_index("gx"), lax.axis_index("gy")
    lane, sub = iota((8, 128), 1), iota((8, 128), 0)
    level = lane % KC

    rhs = [grhs_ref[i] for i in range(zn)]
    pivot = [gpiv_ref[i] for i in range(zn)]

    def sweep(repeat, now):
        new = []
        wrap_low = jnp.where(lane < KC, 0.0, pltpu.roll(now[zn - 1], KC, 1))
        wrap_high = jnp.where(lane >= 128 - KC, 0.0, pltpu.roll(now[0], 128 - KC, 1))
        for i in range(zn):
            value = now[i]
            total = rhs[i] + (now[i - 1] if i > 0 else wrap_low)
            total += now[i + 1] if i < zn - 1 else wrap_high
            total += jnp.where(sub == 0, 0.0, pltpu.roll(value, 1, 0))
            total += jnp.where(sub == 7, 0.0, pltpu.roll(value, 7, 0))
            total += jnp.where(level == 0, 0.0, pltpu.roll(value, 1, 1))
            total += jnp.where(level == KC - 1, 0.0, pltpu.roll(value, 127, 1))
            new.append(total * pivot[i])
        return tuple(new)

    now = lax.fori_loop(0, ITC - 1, sweep, tuple(a * b for a, b in zip(rhs, pivot)))
    for i in range(zn):
        coarse[i] = now[i]

    def table(ax, ay):
        shifted = ax + zn
        value = coarse[shifted % zn]
        value = jnp.where((sub == ay) & (lane // KC == shifted // zn - 1), value, 0.0)
        row = jnp.sum(value, axis=0, keepdims=True)
        row = row + pltpu.roll(row, 64, 1)
        return row + pltpu.roll(row, 32, 1)

    own = table(gx, gy)
    corr_ref[0] = own[:, :KC]
    sides = [table(gx - 1, gy), table(gx + 1, gy), table(gx, gy - 1), table(gx, gy + 1)]
    tables = [jnp.broadcast_to(own, (8, 128))] * 2 + [
        jnp.where(sub < 4, sides[0], sides[1]), jnp.where(sub < 4, sides[2], sides[3])]
    for i in range(4):
        for half in range(2):
            picked = labels[i * 8:i * 8 + 8, half * 128:half * 128 + 128]
            lifted[i * 8:i * 8 + 8, half * 128:half * 128 + 128] = jnp.take_along_axis(
                tables[i], picked, axis=1)
    lifted[32:48, :] = after(lifted[0:16, :])
    lifted[48:64, :] = before(lifted[0:16, :])
    high, low = halves(lifted[...])
    around = jnp.concatenate([high, low, high, low], axis=0)

    def store(x):
        return pltpu.make_async_copy(
            out_v.at[pl.ds(x * SIDE, SIDE)], out_hbm.at[x], out_sem.at[x])

    for x in range(SIDE):
        for y in range(SIDE):
            col = x * SIDE + y
            out_v[col] = base_ref[col] + jnp.dot(coef_ref[col], around, preferred_element_type=f32)
        store(x).start()
    for x in range(SIDE):
        store(x).wait()


def body(gxn, gyn, zn, right_side, diffusivity, agglomerate, element_matrix, face_matrices,
         restriction, prolongation, coarse_shift):
    group = gxn // zn * gyn
    vmem = pl.BlockSpec(memory_space=pltpu.VMEM)
    hbm = pl.BlockSpec(memory_space=pl.ANY)
    dma = pltpu.SemaphoreType.DMA
    field = pltpu.VMEM((COLS, NP, EZ), f32)
    halo = pltpu.VMEM((4, SIDE, NP, EZ), f32)
    parts = pltpu.VMEM((PADS * PADS, NP, EZ), bf16)
    gather = [
        pltpu.VMEM((1, 128), f32),
        pltpu.VMEM((group, 1, 128), f32),
        pltpu.VMEM((8, 128), f32),
        pltpu.VMEM((zn, 8, 128), f32),
    ]
    side_groups = pltpu.VMEM((4, SIDE, 8, EZ), f32)
    side_rows = pltpu.VMEM((4, SIDE, EZ), f32)
    side_labels = pltpu.VMEM((4, SIDE, EZ), jnp.int32)
    base, coef, grhs, gpiv, labels = pl.pallas_call(
        functools.partial(exchange_kernel, gxn, gyn, zn),
        out_shape=(
            jax.ShapeDtypeStruct((COLS, NP, EZ), f32),
            jax.ShapeDtypeStruct((COLS, NP, 256), bf16),
            jax.ShapeDtypeStruct((zn, 8, 128), f32),
            jax.ShapeDtypeStruct((zn, 8, 128), f32),
            jax.ShapeDtypeStruct((2 * COLS, EZ), jnp.int32),
        ),
        in_specs=[pl.BlockSpec(memory_space=pltpu.HBM)] * 8,
        out_specs=(vmem,) * 5,
        scratch_shapes=[
            pltpu.VMEM((SIDE, SIDE, EZ), f32), pltpu.VMEM((SIDE, SIDE, EZ), jnp.int32),
            pltpu.VMEM((NP, NP), f32), pltpu.VMEM((6, NP, NP), f32), pltpu.VMEM((NP,), f32),
            pltpu.VMEM((NP,), f32), pltpu.VMEM((1, 1, KC), f32),
            field, field, field, halo, halo, parts, parts, parts, parts,
            pltpu.VMEM((192, 256), bf16), pltpu.VMEM((128, 256), bf16), pltpu.VMEM((64, 256), bf16),
            field, side_groups, side_groups,
            pltpu.VMEM((COLS, 8, EZ), f32), side_rows, side_rows, side_labels, side_labels,
            *gather, *gather,
            dma((7,)), dma((SIDE,)), dma((4, SIDE)), dma((4, SIDE)), dma((4, SIDE)), dma((4, SIDE)),
            dma((4,)), dma((4,)), dma((4,)), dma((4,)), dma((4,)), dma((4,)), dma((4,)), dma((4,)),
        ],
        compiler_params=pltpu.CompilerParams(
            collective_id=0, has_side_effects=True, vmem_limit_bytes=40 * 2**20),
        name="exchange",
    )(*[pltpu.with_memory_space_constraint(value, pltpu.HBM) for value in (
        right_side, diffusivity, agglomerate, element_matrix, face_matrices, restriction,
        prolongation, coarse_shift)])
    return pl.pallas_call(
        functools.partial(finish_kernel, gxn, gyn, zn),
        out_shape=(
            jax.ShapeDtypeStruct((SIDE, SIDE, NP, EZ), f32),
            jax.ShapeDtypeStruct((1, 1, KC), f32),
        ),
        in_specs=[vmem] * 5,
        out_specs=(hbm, vmem),
        scratch_shapes=[
            field, pltpu.VMEM((zn, 8, 128), f32), pltpu.VMEM((64, EZ), f32), dma((SIDE,)),
        ],
        compiler_params=pltpu.CompilerParams(vmem_limit_bytes=20 * 2**20),
        name="finish",
    )(base, coef, grhs, gpiv, labels)


def solution(mesh):
    gxn, gyn = mesh.shape["gx"], mesh.shape["gy"]
    return jax.shard_map(
        functools.partial(body, gxn, gyn, max(1, gxn // 4)),
        mesh=mesh,
        in_specs=(
            P("gx", "gy", None, None),
            P("gx", "gy", None),
            P("gx", "gy", None),
            P(),
            P(),
            P(),
            P(),
            P("gx", "gy", None),
        ),
        out_specs=(P("gx", "gy", None, None), P("gx", "gy", None)),
        check_vma=False,
    )
```

```python
import functools

import jax
import jax.numpy as jnp
from jax import lax
from jax.experimental import pallas as pl
from jax.experimental.pallas import tpu as pltpu
from jax.sharding import PartitionSpec as P

NP = 64
EZ = 256
KC = 32
ITC = 24
SIDE = 4
COLS = SIDE * SIDE
PADS = SIDE + 2
damping = 0.8
highest = lax.Precision.HIGHEST
MESH = pl.DeviceIdType.MESH
f32, bf16 = jnp.float32, jnp.bfloat16


def halves(values):
    high = values.astype(bf16)
    return high, (values - high.astype(f32)).astype(bf16)


def iota(shape, axis):
    return lax.broadcasted_iota(jnp.int32, shape, axis)


def after(rows):
    return jnp.where(iota(rows.shape, 1) == 0, 0.0, pltpu.roll(rows, 1, 1))


def before(rows):
    last = rows.shape[1] - 1
    return jnp.where(iota(rows.shape, 1) == last, 0.0, pltpu.roll(rows, last, 1))


SOURCE = (
    lambda c: (SIDE - 1) * SIDE + c,
    lambda c: c,
    lambda c: c * SIDE + SIDE - 1,
    lambda c: c * SIDE,
)


def padded_slot(side, c):
    return (c + 1, (PADS - 1) * PADS + c + 1, (c + 1) * PADS, (c + 1) * PADS + PADS - 1)[side]


def exchange_kernel(
    gxn, gyn, zn,
    rhs_hbm, w_hbm, agg_hbm, e_hbm, f_hbm, r_hbm, p_hbm, shift_hbm,
    base_ref, coef_ref, grhs_ref, gpiv_ref, labels_ref,
    w_ref, agg_ref, e_ref, f_ref, r_ref, p_ref, shift_ref, rhs_v, u1, u2, hal1, hal2, p1h, p1l, p2h, p2l, own_w, side_w, path_w,
    field, qsend, qhalo, trow, tsend, thalo, asend, ahalo,
    s1a, r1a, s2a, r2a, s1b, r1b, s2b, r2b,
    small_sem, load_sem, send1, recv1, send2, recv2, tsend_sem, trecv_sem, asend_sem, arecv_sem,
    gsem_a, gsem_b, qsend_sem, qrecv_sem, all_in,
):
    gx, gy = lax.axis_index("gx"), lax.axis_index("gy")
    xg, zg = gx // zn, gx % zn
    xn = gxn // zn
    group = xn * gyn
    mine = xg * gyn + gy
    has = (gx > 0, gx < gxn - 1, gy > 0, gy < gyn - 1)
    sends = (has[1], has[0], has[3], has[2])
    target = ((gx + 1, gy), (gx - 1, gy), (gx, gy + 1), (gx, gy - 1))

    def load(x):
        return pltpu.make_async_copy(
            rhs_hbm.at[x], rhs_v.at[pl.ds(x * SIDE, SIDE)], load_sem.at[x])

    inputs = [
        pltpu.make_async_copy(a, b, small_sem.at[i]) for i, (a, b) in enumerate((
            (e_hbm, e_ref), (f_hbm, f_ref), (r_hbm, r_ref), (p_hbm, p_ref), (w_hbm, w_ref),
            (shift_hbm, shift_ref), (agg_hbm, agg_ref)))]
    for copy in inputs:
        copy.start()
    for x in (0, 3, 1, 2):
        load(x).start()

    barrier = pltpu.get_barrier_semaphore()
    for s in (0, 1):
        @pl.when(sends[s])
        def _(s=s):
            pl.semaphore_signal(barrier, inc=1, device_id=target[s], device_id_type=MESH)

    def greet_plane(j, carry):
        @pl.when(j != mine)
        def _():
            pl.semaphore_signal(
                barrier, inc=1, device_id=((j // gyn) * zn + zg, j % gyn), device_id_type=MESH)
        return carry

    lax.fori_loop(0, group, greet_plane, 0)

    def greet_line(j, carry):
        @pl.when(j != zg)
        def _():
            pl.semaphore_signal(
                barrier, inc=1, device_id=(xg * zn + j, gy), device_id_type=MESH)
        return carry

    lax.fori_loop(0, zn, greet_line, 0)

    for copy in inputs:
        copy.wait()

    same = iota((NP, NP), 0) == iota((NP, NP), 1)
    element = e_ref[...]
    on_diagonal = jnp.where(same, element, 0.0)
    diagonal = jnp.sum(on_diagonal, axis=1, keepdims=True)
    scale = damping / diagonal
    r_row = r_ref[...].reshape(1, NP)
    p_row = p_ref[...].reshape(1, NP)
    r_col = jnp.sum(jnp.where(same, r_row, 0.0), axis=1, keepdims=True)
    p_col = jnp.sum(jnp.where(same, p_row, 0.0), axis=1, keepdims=True)
    faces = [f_ref[d] for d in range(6)]
    scaled = [scale * face for face in faces]
    own_scaled = scale * element
    rows = [jnp.sum(r_col * m, axis=0, keepdims=True) for m in [element] + faces]
    rows.append(r_row * jnp.sum(on_diagonal, axis=0, keepdims=True) / damping)

    def lay(weights, matrix):
        high, low = halves(matrix)
        weights[:, 0:64] = high
        weights[:, 64:128] = high
        weights[:, 128:192] = low
        weights[:, 192:256] = low

    lay(own_w, jnp.concatenate([own_scaled, scaled[4], scaled[5]], axis=0))

    reduce_rows = jnp.concatenate(rows[0:7] + [jnp.zeros((1, NP), f32)], axis=0)
    scaled_rows = reduce_rows * (damping / jnp.sum(on_diagonal, axis=0, keepdims=True))
    products = [jnp.dot(scaled_rows, m, precision=highest, preferred_element_type=f32)
                for m in [element] + faces]
    lay(path_w, jnp.concatenate(
        [2.0 * reduce_rows - products[0]] + products[1:] + [rows[7], jnp.zeros((7, NP), f32)], axis=0))
    for d in range(4):
        high, low = halves(scaled[d])
        side_w[0:64, d * 64:d * 64 + 64] = high
        side_w[64:128, d * 64:d * 64 + 64] = low

    for x in (0, 3, 1, 2):
        load(x).wait()

        def first(y, carry, x=x):
            col = x * SIDE + y
            value = rhs_v[col] * (1.0 / w_ref[x, pl.ds(y, 1), :]) * scale
            u1[col] = value
            slot = (x + 1) * PADS + y + 1
            p1h[slot], p1l[slot] = halves(value)
            return carry

        lax.fori_loop(0, SIDE, first, 0)

    for x in range(SIDE):
        labels_ref[x * SIDE:(x + 1) * SIDE, :] = agg_ref[x]
    asend[0] = agg_ref[SIDE - 1]
    asend[1] = agg_ref[0]
    for c in range(SIDE):
        asend[2, c:c + 1, :] = agg_ref[c, SIDE - 1:SIDE, :]
        asend[3, c:c + 1, :] = agg_ref[c, 0:1, :]

    in_group = iota((1, 128), 1) // KC == xg

    def spread(row):
        return jnp.where(in_group, jnp.concatenate([row] * 4, axis=1), 0.0)

    def follow(x, carry):
        for y in range(SIDE):
            col, slot = x * SIDE + y, (x + 1) * PADS + y + 1
            high, low = p1h[slot], p1l[slot]
            field[col] = jnp.dot(path_w[...], jnp.concatenate([high, low, high, low], axis=0),
                                 preferred_element_type=f32)
        return carry

    lax.fori_loop(0, SIDE, follow, 0)
    for s in range(4):
        for c in range(SIDE):
            qsend[s, c] = field[SOURCE[s](c), 8 + 8 * s:16 + 8 * s, :]

    expected = group - 1 + zn - 1 + has[0].astype(jnp.int32) + has[1].astype(jnp.int32)
    pl.semaphore_wait(barrier, expected)

    def face(values, halo, send, recv, s, c):
        return pltpu.make_async_remote_copy(
            src_ref=values.at[SOURCE[s](c)], dst_ref=halo.at[s, c],
            send_sem=send.at[s, c], recv_sem=recv.at[s, c],
            device_id=target[s], device_id_type=MESH)

    face1 = functools.partial(face, u1, hal1, send1, recv1)
    face2 = functools.partial(face, u2, hal2, send2, recv2)

    def start(make, s, c):
        @pl.when(sends[s])
        def _():
            make(s, c).start()

    def small(values, halo, send, recv, s):
        return pltpu.make_async_remote_copy(
            src_ref=values.at[s], dst_ref=halo.at[s], send_sem=send.at[s], recv_sem=recv.at[s],
            device_id=target[s], device_id_type=MESH)

    paths = functools.partial(small, qsend, qhalo, qsend_sem, qrecv_sem)
    labels = functools.partial(small, asend, ahalo, asend_sem, arecv_sem)
    scalars = functools.partial(small, tsend, thalo, tsend_sem, trecv_sem)

    for s in range(4):
        @pl.when(sends[s])
        def _(s=s):
            paths(s).start()
    for c in range(SIDE):
        for s in (0, 1, 2, 3) if c < 2 else (2, 3):
            start(face1, s, c)

    def gather_first(s1, r1, sems, row):
        s1[...] = row
        r1[mine] = row

        def step(j, carry):
            @pl.when(j != mine)
            def _():
                pltpu.make_async_remote_copy(
                    src_ref=s1, dst_ref=r1.at[mine], send_sem=sems.at[0], recv_sem=sems.at[1],
                    device_id=((j // gyn) * zn + zg, j % gyn), device_id_type=MESH).start()
            return carry

        lax.fori_loop(0, group, step, 0)

    def wait_bytes(ref, count, sem):
        part = ref.at[pl.ds(0, count)]
        pltpu.make_async_copy(part, part, sem).wait()

    def gather_second(r1, s2, r2, sems):
        wait_bytes(r1, group - 1, sems.at[1])
        if gyn < 8:
            s2[...] = jnp.zeros_like(s2)
        for b in range(gyn):
            s2[b:b + 1, :] = sum(r1[q * gyn + b] for q in range(xn))
        r2[zg] = s2[...]

        def step(j, carry):
            @pl.when(j != zg)
            def _():
                pltpu.make_async_remote_copy(
                    src_ref=s2, dst_ref=r2.at[zg], send_sem=sems.at[2], recv_sem=sems.at[3],
                    device_id=(xg * zn + j, gy), device_id_type=MESH).start()
            return carry

        lax.fori_loop(0, zn, step, 0)

    def gather_third(r1, r2, sems, out):
        wait_bytes(r2, zn - 1, sems.at[3])
        out[...] = r2[...]
        wait_bytes(r1, group - 1, sems.at[0])
        wait_bytes(r2, zn - 1, sems.at[2])

    def pass_on(j, carry):
        @pl.when(j != zg)
        def _():
            pl.semaphore_signal(
                all_in, inc=1, device_id=(xg * zn + j, gy), device_id_type=MESH)
        return carry

    lax.fori_loop(0, zn, pass_on, 0)
    core, yg, yn = gy % 2, gy // 2, gyn // 2
    chips = gxn * yn

    def far_first(size):
        half = size // 2
        return [half - (k + 1) // 2 if k % 2 else half + k // 2 for k in range(size)]

    def direct_first(s1, r1, sems, row):
        s1[...] = row
        r1[gx * yn + yg] = row
        pl.semaphore_wait(all_in, zn - 1)

        def send(dx, dy, to_z):
            to_x = (xg + dx) % xn * zn + to_z
            pltpu.make_async_remote_copy(
                src_ref=s1, dst_ref=r1.at[gx * yn + yg], send_sem=sems.at[0], recv_sem=sems.at[1],
                device_id=(to_x, (yg + dy) % yn * 2 + core), device_id_type=MESH).start()

        offsets = [(dx, dy) for dx in far_first(xn) for dy in far_first(yn)]

        def step(k, carry):
            to_z = (zg + jnp.where(k % 2 == 1, zn // 2 - (k + 1) // 2, zn // 2 + k // 2)) % zn
            for dx, dy in offsets:
                send(dx, dy, to_z)
            return carry

        lax.fori_loop(0, zn - 1, step, 0)
        for dx, dy in offsets[:-1]:
            send(dx, dy, zg)

    def pair(s2, r2, sems):
        return pltpu.make_async_remote_copy(
            src_ref=s2, dst_ref=r2, send_sem=sems.at[2], recv_sem=sems.at[3],
            device_id=(gx, gy + 1 - 2 * core), device_id_type=MESH)

    def direct_second(r1, s2, r2, sems):
        wait_bytes(r1, chips - 1, sems.at[1])
        s2[...] = jnp.zeros_like(s2)
        for i in range(zn):
            for y in range(yn):
                s2[i, pl.ds(2 * y + core, 1), :] = sum(
                    r1[(q * zn + i) * yn + y] for q in range(xn))
        pair(s2, r2, sems).start()

    def direct_third(r1, s2, r2, sems, out):
        pair(s2, r2, sems).wait_recv()
        out[...] = s2[...] + r2[...]
        wait_bytes(r1, chips - 1, sems.at[0])
        pair(s2, r2, sems).wait_send()

    gather_first(s1a, r1a, gsem_a, spread(1.0 / (6.0 + shift_ref[0])))

    nothing = jnp.zeros((NP, EZ), bf16)
    for s in range(4):
        @pl.when(jnp.logical_not(has[s]))
        def _(s=s):
            thalo[s] = jnp.zeros((SIDE, EZ), f32)
            qhalo[s] = jnp.zeros((SIDE, 8, EZ), f32)
            ahalo[s] = jnp.zeros((SIDE, EZ), jnp.int32)
            for c in range(SIDE):
                slot = padded_slot(s, c)
                p1h[slot] = nothing
                p1l[slot] = nothing
                p2h[slot] = nothing
                p2l[slot] = nothing

    own_matrix = own_w
    side_matrix = side_w

    def own_part(high_ref, low_ref, slot):
        high, low = high_ref[slot], low_ref[slot]
        g = jnp.dot(own_matrix[...], jnp.concatenate([high, low, high, low], axis=0),
                    preferred_element_type=f32)
        return g[0:64] - after(g[64:128]) - before(g[128:192])

    def side_part(high_ref, low_ref, slot):
        around = (slot - PADS, slot + PADS, slot - 1, slot + 1)
        high = jnp.concatenate([high_ref[s] for s in around], axis=0)
        low = jnp.concatenate([low_ref[s] for s in around], axis=0)
        both = jnp.dot(side_matrix[...], high, preferred_element_type=f32)
        return both[0:64] + both[64:128] + jnp.dot(
            side_matrix[0:64, :], low, preferred_element_type=f32)

    def second(x, y):
        col, slot = x * SIDE + y, (x + 1) * PADS + y + 1
        before_it = u1[col]
        value = 2.0 * before_it - own_part(p1h, p1l, slot) + side_part(p1h, p1l, slot)
        u2[col] = value
        p2h[slot], p2l[slot] = halves(value)

    def second_own(x, y):
        col, slot = x * SIDE + y, (x + 1) * PADS + y + 1
        base_ref[col] = u2[col] + u1[col] - own_part(p2h, p2l, slot)

    def arrive(make, halo, high_ref, low_ref, s, c):
        @pl.when(has[s])
        def _():
            make(s, c).wait_recv()
            slot = padded_slot(s, c)
            high_ref[slot], low_ref[slot] = halves(halo[s, c])

    arrive1 = functools.partial(arrive, face1, hal1, p1h, p1l)
    arrive2 = functools.partial(arrive, face2, hal2, p2h, p2l)

    def interior(i, carry):
        second(1, i + 1)
        second(2, i + 1)
        second_own(1, i + 1)
        second_own(2, i + 1)
        return carry

    lax.fori_loop(0, 2, interior, 0)

    for s in range(4):
        @pl.when(has[s])
        def _(s=s):
            paths(s).wait_recv()
    for x in range(SIDE):
        for y in range(SIDE):
            col = x * SIDE + y
            value = field[col, 0:8, :] + after(field[col, 40:48, :]) + before(field[col, 48:56, :])
            value += field[col - SIDE, 8:16, :] if x > 0 else qhalo[0, y]
            value += field[col + SIDE, 16:24, :] if x < SIDE - 1 else qhalo[1, y]
            value += field[col - 1, 24:32, :] if y > 0 else qhalo[2, x]
            value += field[col + 1, 32:40, :] if y < SIDE - 1 else qhalo[3, x]
            total = field[col, 56:57, :] - value[0:1] + after(value[5:6]) + before(value[6:7])
            trow[col] = jnp.where(iota((8, EZ), 0) == 0, total, value)
    for s in range(4):
        for c in range(SIDE):
            tsend[s, c:c + 1, :] = trow[SOURCE[s](c), s + 1:s + 2, :]

        @pl.when(sends[s])
        def _(s=s):
            scalars(s).start()
    for c in range(2, SIDE):
        for s in (0, 1):
            start(face1, s, c)
    for s in range(4):
        @pl.when(sends[s])
        def _(s=s):
            labels(s).start()

    for c in range(SIDE):
        for s in (2, 3):
            arrive1(s, c)
    gather_second(r1a, s2a, r2a, gsem_a)

    def side_y(i, carry):
        second(i + 1, 0)
        second(i + 1, SIDE - 1)
        second_own(i + 1, 0)
        second_own(i + 1, SIDE - 1)
        return carry

    lax.fori_loop(0, 2, side_y, 0)
    for c in (1, 2):
        for s in (2, 3):
            start(face2, s, c)

    for s in range(4):
        @pl.when(has[s])
        def _(s=s):
            scalars(s).wait_recv()

    levels = iota((KC, EZ), 0)
    total = jnp.zeros((KC, EZ), f32)
    for x in range(SIDE):
        for y in range(SIDE):
            col = x * SIDE + y
            row = trow[col, 0:1, :]
            row += trow[col - SIDE, 1:2, :] if x > 0 else thalo[0, y:y + 1, :]
            row += trow[col + SIDE, 2:3, :] if x < SIDE - 1 else thalo[1, y:y + 1, :]
            row += trow[col - 1, 3:4, :] if y > 0 else thalo[2, x:x + 1, :]
            row += trow[col + 1, 4:5, :] if y < SIDE - 1 else thalo[3, x:x + 1, :]
            row = row * w_ref[x, y:y + 1, :]
            total += jnp.where(agg_ref[x, y:y + 1, :] == levels, row, 0.0)
    sums = lax.dot_general(
        jnp.ones((8, EZ), f32), jnp.concatenate([total] * 4, axis=0),
        (((1,), (1,)), ((), ())), precision=highest, preferred_element_type=f32)
    direct_first(s1b, r1b, gsem_b, jnp.where(in_group, sums[0:1], 0.0))

    for c in range(SIDE):
        arrive1(0, c)
        arrive1(1, c)
        second(0, c)
        second(SIDE - 1, c)
        start(face2, 0, c)
        start(face2, 1, c)
        if c in (0, SIDE - 1):
            s = 3 if c == 0 else 2
            start(face2, s, 0)
            start(face2, s, SIDE - 1)
        second_own(0, c)
        second_own(SIDE - 1, c)

    direct_second(r1b, s2b, r2b, gsem_b)

    def last(x, y):
        col, slot = x * SIDE + y, (x + 1) * PADS + y + 1
        base_ref[col] += side_part(p2h, p2l, slot)

    def last_interior(i, carry):
        last(1, i + 1)
        last(2, i + 1)
        return carry

    lax.fori_loop(0, 2, last_interior, 0)

    for c in range(SIDE):
        for s in (2, 3):
            arrive2(s, c)

    def last_y(i, carry):
        last(i + 1, 0)
        last(i + 1, SIDE - 1)
        return carry

    lax.fori_loop(0, 2, last_y, 0)

    gains = [jnp.sum(m * p_row, axis=1, keepdims=True) for m in scaled]
    own_gain = p_col - jnp.sum(own_scaled * p_row, axis=1, keepdims=True)
    lane = iota((NP, 256), 1)
    at = lane % 64

    def coefficients(col, carry):
        x, y = col // SIDE, col % SIDE
        places = (
            jnp.where(x > 0, col - SIDE, COLS + y),
            jnp.where(x < SIDE - 1, col + SIDE, COLS + SIDE + y),
            jnp.where(y > 0, col - 1, COLS + 2 * SIDE + x),
            jnp.where(y < SIDE - 1, col + 1, COLS + 3 * SIDE + x),
            2 * COLS + col,
            3 * COLS + col,
        )
        matrix = jnp.where(at == col, own_gain, 0.0)
        for d in range(6):
            matrix = jnp.where(at == places[d], gains[d], matrix)
        high, low = halves(matrix)
        coef_ref[col] = jnp.where(lane < 128, high.astype(f32), low.astype(f32)).astype(bf16)
        return carry

    lax.fori_loop(0, COLS, coefficients, 0)

    for c in range(SIDE):
        arrive2(0, c)
        arrive2(1, c)
        last(0, c)
        last(SIDE - 1, c)

    for s in range(4):
        @pl.when(has[s])
        def _(s=s):
            labels(s).wait_recv()
    for s in range(4):
        labels_ref[COLS + s * SIDE:COLS + (s + 1) * SIDE, :] = ahalo[s]
    gather_third(r1a, r2a, gsem_a, gpiv_ref)
    direct_third(r1b, s2b, r2b, gsem_b, grhs_ref)

    for s in range(4):
        @pl.when(sends[s])
        def _(s=s):
            labels(s).wait_send()
            scalars(s).wait_send()
            paths(s).wait_send()
            for c in range(SIDE):
                face1(s, c).wait_send()
                face2(s, c).wait_send()


def finish_kernel(
    gxn, gyn, zn,
    base_ref, coef_ref, grhs_ref, gpiv_ref, labels,
    out_hbm, corr_ref,
    out_v, coarse, lifted, out_sem,
):
    gx, gy = lax.axis_index("gx"), lax.axis_index("gy")
    lane, sub = iota((8, 128), 1), iota((8, 128), 0)
    level = lane % KC

    rhs = [grhs_ref[i] for i in range(zn)]
    pivot = [gpiv_ref[i] for i in range(zn)]

    def sweep(repeat, now):
        new = []
        wrap_low = jnp.where(lane < KC, 0.0, pltpu.roll(now[zn - 1], KC, 1))
        wrap_high = jnp.where(lane >= 128 - KC, 0.0, pltpu.roll(now[0], 128 - KC, 1))
        for i in range(zn):
            value = now[i]
            total = rhs[i] + (now[i - 1] if i > 0 else wrap_low)
            total += now[i + 1] if i < zn - 1 else wrap_high
            total += jnp.where(sub == 0, 0.0, pltpu.roll(value, 1, 0))
            total += jnp.where(sub == 7, 0.0, pltpu.roll(value, 7, 0))
            total += jnp.where(level == 0, 0.0, pltpu.roll(value, 1, 1))
            total += jnp.where(level == KC - 1, 0.0, pltpu.roll(value, 127, 1))
            new.append(total * pivot[i])
        return tuple(new)

    now = lax.fori_loop(0, ITC - 1, sweep, tuple(a * b for a, b in zip(rhs, pivot)))
    for i in range(zn):
        coarse[i] = now[i]

    def table(ax, ay):
        shifted = ax + zn
        value = coarse[shifted % zn]
        value = jnp.where((sub == ay) & (lane // KC == shifted // zn - 1), value, 0.0)
        row = jnp.sum(value, axis=0, keepdims=True)
        row = row + pltpu.roll(row, 64, 1)
        return row + pltpu.roll(row, 32, 1)

    own = table(gx, gy)
    corr_ref[0] = own[:, :KC]
    sides = [table(gx - 1, gy), table(gx + 1, gy), table(gx, gy - 1), table(gx, gy + 1)]
    tables = [jnp.broadcast_to(own, (8, 128))] * 2 + [
        jnp.where(sub < 4, sides[0], sides[1]), jnp.where(sub < 4, sides[2], sides[3])]
    for i in range(4):
        for half in range(2):
            picked = labels[i * 8:i * 8 + 8, half * 128:half * 128 + 128]
            lifted[i * 8:i * 8 + 8, half * 128:half * 128 + 128] = jnp.take_along_axis(
                tables[i], picked, axis=1)
    lifted[32:48, :] = after(lifted[0:16, :])
    lifted[48:64, :] = before(lifted[0:16, :])
    high, low = halves(lifted[...])
    around = jnp.concatenate([high, low, high, low], axis=0)

    def store(x):
        return pltpu.make_async_copy(
            out_v.at[pl.ds(x * SIDE, SIDE)], out_hbm.at[x], out_sem.at[x])

    for x in range(SIDE):
        for y in range(SIDE):
            col = x * SIDE + y
            out_v[col] = base_ref[col] + jnp.dot(coef_ref[col], around, preferred_element_type=f32)
        store(x).start()
    for x in range(SIDE):
        store(x).wait()


def body(gxn, gyn, zn, right_side, diffusivity, agglomerate, element_matrix, face_matrices,
         restriction, prolongation, coarse_shift):
    group = gxn // zn * gyn
    vmem = pl.BlockSpec(memory_space=pltpu.VMEM)
    hbm = pl.BlockSpec(memory_space=pl.ANY)
    dma = pltpu.SemaphoreType.DMA
    field = pltpu.VMEM((COLS, NP, EZ), f32)
    halo = pltpu.VMEM((4, SIDE, NP, EZ), f32)
    parts = pltpu.VMEM((PADS * PADS, NP, EZ), bf16)
    gather = [
        pltpu.VMEM((1, 128), f32),
        pltpu.VMEM((group, 1, 128), f32),
        pltpu.VMEM((8, 128), f32),
        pltpu.VMEM((zn, 8, 128), f32),
    ]
    direct = [
        pltpu.VMEM((1, 128), f32),
        pltpu.VMEM((gxn * gyn // 2, 1, 128), f32),
        pltpu.VMEM((zn, 8, 128), f32),
        pltpu.VMEM((zn, 8, 128), f32),
    ]
    side_groups = pltpu.VMEM((4, SIDE, 8, EZ), f32)
    side_rows = pltpu.VMEM((4, SIDE, EZ), f32)
    side_labels = pltpu.VMEM((4, SIDE, EZ), jnp.int32)
    base, coef, grhs, gpiv, labels = pl.pallas_call(
        functools.partial(exchange_kernel, gxn, gyn, zn),
        out_shape=(
            jax.ShapeDtypeStruct((COLS, NP, EZ), f32),
            jax.ShapeDtypeStruct((COLS, NP, 256), bf16),
            jax.ShapeDtypeStruct((zn, 8, 128), f32),
            jax.ShapeDtypeStruct((zn, 8, 128), f32),
            jax.ShapeDtypeStruct((2 * COLS, EZ), jnp.int32),
        ),
        in_specs=[pl.BlockSpec(memory_space=pltpu.HBM)] * 8,
        out_specs=(vmem,) * 5,
        scratch_shapes=[
            pltpu.VMEM((SIDE, SIDE, EZ), f32), pltpu.VMEM((SIDE, SIDE, EZ), jnp.int32),
            pltpu.VMEM((NP, NP), f32), pltpu.VMEM((6, NP, NP), f32), pltpu.VMEM((NP,), f32),
            pltpu.VMEM((NP,), f32), pltpu.VMEM((1, 1, KC), f32),
            field, field, field, halo, halo, parts, parts, parts, parts,
            pltpu.VMEM((192, 256), bf16), pltpu.VMEM((128, 256), bf16), pltpu.VMEM((64, 256), bf16),
            field, side_groups, side_groups,
            pltpu.VMEM((COLS, 8, EZ), f32), side_rows, side_rows, side_labels, side_labels,
            *gather, *direct,
            dma((7,)), dma((SIDE,)), dma((4, SIDE)), dma((4, SIDE)), dma((4, SIDE)), dma((4, SIDE)),
            *[dma((4,))] * 8, pltpu.SemaphoreType.REGULAR,
        ],
        compiler_params=pltpu.CompilerParams(
            collective_id=0, has_side_effects=True, vmem_limit_bytes=40 * 2**20),
        name="exchange",
    )(*[pltpu.with_memory_space_constraint(value, pltpu.HBM) for value in (
        right_side, diffusivity, agglomerate, element_matrix, face_matrices, restriction,
        prolongation, coarse_shift)])
    return pl.pallas_call(
        functools.partial(finish_kernel, gxn, gyn, zn),
        out_shape=(
            jax.ShapeDtypeStruct((SIDE, SIDE, NP, EZ), f32),
            jax.ShapeDtypeStruct((1, 1, KC), f32),
        ),
        in_specs=[vmem] * 5,
        out_specs=(hbm, vmem),
        scratch_shapes=[
            field, pltpu.VMEM((zn, 8, 128), f32), pltpu.VMEM((64, EZ), f32), dma((SIDE,)),
        ],
        compiler_params=pltpu.CompilerParams(vmem_limit_bytes=20 * 2**20),
        name="finish",
    )(base, coef, grhs, gpiv, labels)


def solution(mesh):
    gxn, gyn = mesh.shape["gx"], mesh.shape["gy"]
    return jax.shard_map(
        functools.partial(body, gxn, gyn, max(1, gxn // 4)),
        mesh=mesh,
        in_specs=(
            P("gx", "gy", None, None),
            P("gx", "gy", None),
            P("gx", "gy", None),
            P(),
            P(),
            P(),
            P(),
            P("gx", "gy", None),
        ),
        out_specs=(P("gx", "gy", None, None), P("gx", "gy", None)),
        check_vma=False,
    )
```

```python
import functools

import jax
import jax.numpy as jnp
from jax import lax
from jax.experimental import pallas as pl
from jax.experimental.pallas import tpu as pltpu
from jax.sharding import PartitionSpec as P

NP = 64
EZ = 256
KC = 32
ITC = 24
SIDE = 4
COLS = SIDE * SIDE
PADS = SIDE + 2
damping = 0.8
highest = lax.Precision.HIGHEST
MESH = pl.DeviceIdType.MESH
f32, bf16 = jnp.float32, jnp.bfloat16


def halves(values):
    high = values.astype(bf16)
    return high, (values - high.astype(f32)).astype(bf16)


def iota(shape, axis):
    return lax.broadcasted_iota(jnp.int32, shape, axis)


def after(rows):
    return jnp.where(iota(rows.shape, 1) == 0, 0.0, pltpu.roll(rows, 1, 1))


def before(rows):
    last = rows.shape[1] - 1
    return jnp.where(iota(rows.shape, 1) == last, 0.0, pltpu.roll(rows, last, 1))


SOURCE = (
    lambda c: (SIDE - 1) * SIDE + c,
    lambda c: c,
    lambda c: c * SIDE + SIDE - 1,
    lambda c: c * SIDE,
)


def padded_slot(side, c):
    return (c + 1, (PADS - 1) * PADS + c + 1, (c + 1) * PADS, (c + 1) * PADS + PADS - 1)[side]


def exchange_kernel(
    gxn, gyn, zn,
    rhs_hbm, w_hbm, agg_hbm, e_hbm, f_hbm, r_hbm, p_hbm, shift_hbm,
    base_ref, coef_ref, grhs_ref, gpiv_ref, labels_ref,
    w_ref, agg_ref, e_ref, f_ref, r_ref, p_ref, shift_ref, rhs_v, u1, u2, hal1, hal2, p1h, p1l, p2h, p2l, own_w, side_w, path_w,
    field, qsend, qhalo, trow, asend, ahalo, placed, sib_out, sib_in,
    s1a, r1a, s2a, r2a, s1b, r1b, s2b, r2b,
    small_sem, load_sem, send1, recv1, send2, recv2, asend_sem, arecv_sem,
    gsem_a, gsem_b, qsend_sem, qrecv_sem, sib_sem, all_in,
):
    gx, gy = lax.axis_index("gx"), lax.axis_index("gy")
    xg, zg = gx // zn, gx % zn
    xn = gxn // zn
    group = xn * gyn
    mine = xg * gyn + gy
    has = (gx > 0, gx < gxn - 1, gy > 0, gy < gyn - 1)
    sends = (has[1], has[0], has[3], has[2])
    target = ((gx + 1, gy), (gx - 1, gy), (gx, gy + 1), (gx, gy - 1))

    def load(x):
        return pltpu.make_async_copy(
            rhs_hbm.at[x], rhs_v.at[pl.ds(x * SIDE, SIDE)], load_sem.at[x])

    inputs = [
        pltpu.make_async_copy(a, b, small_sem.at[i]) for i, (a, b) in enumerate((
            (e_hbm, e_ref), (f_hbm, f_ref), (r_hbm, r_ref), (p_hbm, p_ref), (w_hbm, w_ref),
            (shift_hbm, shift_ref), (agg_hbm, agg_ref)))]
    for copy in inputs:
        copy.start()
    for x in (0, 3, 1, 2):
        load(x).start()

    barrier = pltpu.get_barrier_semaphore()
    for s in (0, 1):
        @pl.when(sends[s])
        def _(s=s):
            pl.semaphore_signal(barrier, inc=1, device_id=target[s], device_id_type=MESH)

    def greet_plane(j, carry):
        @pl.when(j != mine)
        def _():
            pl.semaphore_signal(
                barrier, inc=1, device_id=((j // gyn) * zn + zg, j % gyn), device_id_type=MESH)
        return carry

    lax.fori_loop(0, group, greet_plane, 0)

    def greet_line(j, carry):
        @pl.when(j != zg)
        def _():
            pl.semaphore_signal(
                barrier, inc=1, device_id=(xg * zn + j, gy), device_id_type=MESH)
        return carry

    lax.fori_loop(0, zn, greet_line, 0)

    for copy in inputs:
        copy.wait()

    same = iota((NP, NP), 0) == iota((NP, NP), 1)
    element = e_ref[...]
    on_diagonal = jnp.where(same, element, 0.0)
    diagonal = jnp.sum(on_diagonal, axis=1, keepdims=True)
    scale = damping / diagonal
    r_row = r_ref[...].reshape(1, NP)
    p_row = p_ref[...].reshape(1, NP)
    r_col = jnp.sum(jnp.where(same, r_row, 0.0), axis=1, keepdims=True)
    p_col = jnp.sum(jnp.where(same, p_row, 0.0), axis=1, keepdims=True)
    faces = [f_ref[d] for d in range(6)]
    scaled = [scale * face for face in faces]
    own_scaled = scale * element
    rows = [jnp.sum(r_col * m, axis=0, keepdims=True) for m in [element] + faces]
    rows.append(r_row * jnp.sum(on_diagonal, axis=0, keepdims=True) / damping)

    def lay(weights, matrix):
        high, low = halves(matrix)
        weights[:, 0:64] = high
        weights[:, 64:128] = high
        weights[:, 128:192] = low
        weights[:, 192:256] = low

    lay(own_w, jnp.concatenate([own_scaled, scaled[4], scaled[5]], axis=0))

    reduce_rows = jnp.concatenate(rows[0:7] + [jnp.zeros((1, NP), f32)], axis=0)
    scaled_rows = reduce_rows * (damping / jnp.sum(on_diagonal, axis=0, keepdims=True))
    products = [jnp.dot(scaled_rows, m, precision=highest, preferred_element_type=f32)
                for m in [element] + faces]
    lay(path_w, jnp.concatenate(
        [2.0 * reduce_rows - products[0]] + products[1:] + [rows[7], jnp.zeros((7, NP), f32)], axis=0))
    for d in range(4):
        high, low = halves(scaled[d])
        side_w[0:64, d * 64:d * 64 + 64] = high
        side_w[64:128, d * 64:d * 64 + 64] = low

    for x in (0, 3, 1, 2):
        load(x).wait()

        def first(y, carry, x=x):
            col = x * SIDE + y
            value = rhs_v[col] * (1.0 / w_ref[x, pl.ds(y, 1), :]) * scale
            u1[col] = value
            slot = (x + 1) * PADS + y + 1
            p1h[slot], p1l[slot] = halves(value)
            return carry

        lax.fori_loop(0, SIDE, first, 0)

    for x in range(SIDE):
        labels_ref[x * SIDE:(x + 1) * SIDE, :] = agg_ref[x].astype(f32)
    for s in range(4):
        for c in range(SIDE):
            x, y = SOURCE[s](c) // SIDE, SOURCE[s](c) % SIDE
            asend[s, c:c + 1, :] = w_ref[x, y:y + 1, :]
            asend[s, SIDE + c:SIDE + c + 1, :] = agg_ref[x, y:y + 1, :].astype(f32)
    placed[...] = jnp.zeros_like(placed)

    in_group = iota((1, 128), 1) // KC == xg

    def spread(row):
        return jnp.where(in_group, jnp.concatenate([row] * 4, axis=1), 0.0)

    def follow(x, carry):
        for y in range(SIDE):
            col, slot = x * SIDE + y, (x + 1) * PADS + y + 1
            high, low = p1h[slot], p1l[slot]
            field[col] = jnp.dot(path_w[...], jnp.concatenate([high, low, high, low], axis=0),
                                 preferred_element_type=f32)
        return carry

    lax.fori_loop(0, SIDE, follow, 0)
    for s in range(4):
        for c in range(SIDE):
            qsend[s, c] = field[SOURCE[s](c), 8 + 8 * s:16 + 8 * s, :]

    expected = group - 1 + zn - 1 + has[0].astype(jnp.int32) + has[1].astype(jnp.int32)
    pl.semaphore_wait(barrier, expected)

    def face(values, halo, send, recv, s, c):
        return pltpu.make_async_remote_copy(
            src_ref=values.at[SOURCE[s](c)], dst_ref=halo.at[s, c],
            send_sem=send.at[s, c], recv_sem=recv.at[s, c],
            device_id=target[s], device_id_type=MESH)

    face1 = functools.partial(face, u1, hal1, send1, recv1)
    face2 = functools.partial(face, u2, hal2, send2, recv2)

    def start(make, s, c):
        @pl.when(sends[s])
        def _():
            make(s, c).start()

    def small(values, halo, send, recv, s):
        return pltpu.make_async_remote_copy(
            src_ref=values.at[s], dst_ref=halo.at[s], send_sem=send.at[s], recv_sem=recv.at[s],
            device_id=target[s], device_id_type=MESH)

    paths = functools.partial(small, qsend, qhalo, qsend_sem, qrecv_sem)
    labels = functools.partial(small, asend, ahalo, asend_sem, arecv_sem)

    for s in range(4):
        @pl.when(sends[s])
        def _(s=s):
            paths(s).start()
            labels(s).start()
    for c in range(SIDE):
        for s in (0, 1, 2, 3) if c < SIDE - 1 else (2, 3):
            start(face1, s, c)

    def gather_first(s1, r1, sems, row):
        s1[...] = row
        r1[mine] = row

        def step(j, carry):
            @pl.when(j != mine)
            def _():
                pltpu.make_async_remote_copy(
                    src_ref=s1, dst_ref=r1.at[mine], send_sem=sems.at[0], recv_sem=sems.at[1],
                    device_id=((j // gyn) * zn + zg, j % gyn), device_id_type=MESH).start()
            return carry

        lax.fori_loop(0, group, step, 0)

    def wait_bytes(ref, count, sem):
        part = ref.at[pl.ds(0, count)]
        pltpu.make_async_copy(part, part, sem).wait()

    def gather_second(r1, s2, r2, sems):
        wait_bytes(r1, group - 1, sems.at[1])
        if gyn < 8:
            s2[...] = jnp.zeros_like(s2)
        for b in range(gyn):
            s2[b:b + 1, :] = sum(r1[q * gyn + b] for q in range(xn))
        r2[zg] = s2[...]

        def step(j, carry):
            @pl.when(j != zg)
            def _():
                pltpu.make_async_remote_copy(
                    src_ref=s2, dst_ref=r2.at[zg], send_sem=sems.at[2], recv_sem=sems.at[3],
                    device_id=(xg * zn + j, gy), device_id_type=MESH).start()
            return carry

        lax.fori_loop(0, zn, step, 0)

    def gather_third(r1, r2, sems, out):
        wait_bytes(r2, zn - 1, sems.at[3])
        out[...] = r2[...]
        wait_bytes(r1, group - 1, sems.at[0])
        wait_bytes(r2, zn - 1, sems.at[2])

    def pass_on(j, carry):
        @pl.when(j != zg)
        def _():
            pl.semaphore_signal(
                all_in, inc=1, device_id=(xg * zn + j, gy), device_id_type=MESH)
        return carry

    lax.fori_loop(0, zn, pass_on, 0)
    core, yg, yn = gy % 2, gy // 2, gyn // 2
    chips = gxn * yn

    def far_first(size):
        half = size // 2
        return [half - (k + 1) // 2 if k % 2 else half + k // 2 for k in range(size)]

    def direct_first(rows):
        s1b[...] = rows
        r1b[gx * yn + yg] = rows
        pl.semaphore_wait(all_in, zn - 1)

        def send(dx, dy, to_z):
            to_x = (xg + dx) % xn * zn + to_z
            pltpu.make_async_remote_copy(
                src_ref=s1b, dst_ref=r1b.at[gx * yn + yg], send_sem=gsem_b.at[0],
                recv_sem=gsem_b.at[1],
                device_id=(to_x, (yg + dy) % yn * 2 + core), device_id_type=MESH).start()

        offsets = [(dx, dy) for dx in far_first(xn) for dy in far_first(yn)]

        def step(k, carry):
            to_z = (zg + jnp.where(k % 2 == 1, zn // 2 - (k + 1) // 2, zn // 2 + k // 2)) % zn
            for dx, dy in offsets:
                send(dx, dy, to_z)
            return carry

        lax.fori_loop(0, zn - 1, step, 0)
        for dx, dy in offsets[:-1]:
            send(dx, dy, zg)

    pair = pltpu.make_async_remote_copy(
        src_ref=s2b, dst_ref=r2b, send_sem=gsem_b.at[2], recv_sem=gsem_b.at[3],
        device_id=(gx, gy + 1 - 2 * core), device_id_type=MESH)

    def direct_second():
        wait_bytes(r1b, chips - 1, gsem_b.at[1])
        for q in range(xn):
            for i in range(zn):
                for y in range(yn):
                    at = (q * zn + i) * yn + y
                    placed[q, i, pl.ds(2 * y + core, 1), :] = r1b[at]
        kind, sub = iota((8, 128), 1) // KC, iota((8, 128), 0)
        zero = jnp.zeros((8, 128), f32)
        step_y, edge = jnp.where(core == 1, 1, 7), jnp.where(core == 1, 0, 7)

        def source(q, i):
            return placed[q, i] if q < xn else zero

        for i in range(zn):
            total = zero
            for r in range(4):
                own = source(r, i)
                if i > 0:
                    left = source((1 + r) % 4, i - 1)
                else:
                    left = source(r, zn - 1) if r < 3 else zero
                if i < zn - 1:
                    right = source((2 + r) % 4, i + 1)
                else:
                    right = source((3 + r) % 4, 0) if (3 + r) % 4 else zero
                beside = jnp.where(
                    sub == edge, 0.0, pltpu.roll(source((3 + r) % 4, i), step_y, 0))
                moved = jnp.where(kind < 2, jnp.where(kind == 0, own, left),
                                  jnp.where(kind == 2, right, beside))
                total += pltpu.roll(moved, KC * r, 1) if r else moved
            s2b[i] = total
        pair.start()

    def direct_third(out):
        pair.wait_recv()
        out[...] = s2b[...] + r2b[...]
        wait_bytes(r1b, chips - 1, gsem_b.at[0])
        pair.wait_send()
        sib_copy.wait_send()

    gather_first(s1a, r1a, gsem_a, spread(1.0 / (6.0 + shift_ref[0])))

    nothing = jnp.zeros((NP, EZ), bf16)
    for s in range(4):
        @pl.when(jnp.logical_not(has[s]))
        def _(s=s):
            qhalo[s] = jnp.zeros((SIDE, 8, EZ), f32)
            ahalo[s] = jnp.zeros((2 * SIDE, EZ), f32)
            for c in range(SIDE):
                slot = padded_slot(s, c)
                p1h[slot] = nothing
                p1l[slot] = nothing
                p2h[slot] = nothing
                p2l[slot] = nothing

    own_matrix = own_w
    side_matrix = side_w

    def own_part(high_ref, low_ref, slot):
        high, low = high_ref[slot], low_ref[slot]
        g = jnp.dot(own_matrix[...], jnp.concatenate([high, low, high, low], axis=0),
                    preferred_element_type=f32)
        return g[0:64] - after(g[64:128]) - before(g[128:192])

    def side_part(high_ref, low_ref, slot):
        around = (slot - PADS, slot + PADS, slot - 1, slot + 1)
        high = jnp.concatenate([high_ref[s] for s in around], axis=0)
        low = jnp.concatenate([low_ref[s] for s in around], axis=0)
        both = jnp.dot(side_matrix[...], high, preferred_element_type=f32)
        return both[0:64] + both[64:128] + jnp.dot(
            side_matrix[0:64, :], low, preferred_element_type=f32)

    def second(x, y):
        col, slot = x * SIDE + y, (x + 1) * PADS + y + 1
        before_it = u1[col]
        value = 2.0 * before_it - own_part(p1h, p1l, slot) + side_part(p1h, p1l, slot)
        u2[col] = value
        p2h[slot], p2l[slot] = halves(value)

    def second_own(x, y):
        col, slot = x * SIDE + y, (x + 1) * PADS + y + 1
        base_ref[col] = u2[col] + u1[col] - own_part(p2h, p2l, slot)

    def arrive(make, halo, high_ref, low_ref, s, c):
        @pl.when(has[s])
        def _():
            make(s, c).wait_recv()
            slot = padded_slot(s, c)
            high_ref[slot], low_ref[slot] = halves(halo[s, c])

    arrive1 = functools.partial(arrive, face1, hal1, p1h, p1l)
    arrive2 = functools.partial(arrive, face2, hal2, p2h, p2l)

    def interior(i, carry):
        second(1, i + 1)
        second(2, i + 1)
        second_own(1, i + 1)
        second_own(2, i + 1)
        return carry

    lax.fori_loop(0, 2, interior, 0)

    for s in range(4):
        @pl.when(has[s])
        def _(s=s):
            paths(s).wait_recv()
            labels(s).wait_recv()
    for x in range(SIDE):
        for y in range(SIDE):
            col = x * SIDE + y
            value = field[col, 0:8, :] + after(field[col, 40:48, :]) + before(field[col, 48:56, :])
            value += field[col - SIDE, 8:16, :] if x > 0 else qhalo[0, y]
            value += field[col + SIDE, 16:24, :] if x < SIDE - 1 else qhalo[1, y]
            value += field[col - 1, 24:32, :] if y > 0 else qhalo[2, x]
            value += field[col + 1, 32:40, :] if y < SIDE - 1 else qhalo[3, x]
            total = field[col, 56:57, :] - value[0:1] + after(value[5:6]) + before(value[6:7])
            trow[col] = jnp.where(iota((8, EZ), 0) == 0, total, value)

    for s in range(4):
        labels_ref[COLS + s * SIDE:COLS + (s + 1) * SIDE, :] = ahalo[s, SIDE:2 * SIDE, :]
    levels = iota((KC, EZ), 0)
    float_levels = levels.astype(f32)

    def to_side(s):
        total = jnp.zeros((KC, EZ), f32)
        side = s + 1 - 2 * (s % 2)
        for c in range(SIDE):
            row = trow[SOURCE[s](c), s + 1:s + 2, :] * ahalo[side, c:c + 1, :]
            total += jnp.where(ahalo[side, SIDE + c:SIDE + c + 1, :] == float_levels, row, 0.0)
        return total

    up, down = to_side(2), to_side(3)
    sib_out[...] = jnp.where(core == 0, up, down)
    sib_copy = pltpu.make_async_remote_copy(
        src_ref=sib_out, dst_ref=sib_in, send_sem=sib_sem.at[0], recv_sem=sib_sem.at[1],
        device_id=(gx, gy + 1 - 2 * core), device_id_type=MESH)
    sib_copy.start()
    total = jnp.zeros((KC, EZ), f32)
    for x in range(SIDE):
        for y in range(SIDE):
            col = x * SIDE + y
            row = trow[col, 0:1, :]
            if x > 0:
                row += trow[col - SIDE, 1:2, :]
            if x < SIDE - 1:
                row += trow[col + SIDE, 2:3, :]
            if y > 0:
                row += trow[col - 1, 3:4, :]
            if y < SIDE - 1:
                row += trow[col + 1, 4:5, :]
            row = row * w_ref[x, y:y + 1, :]
            total += jnp.where(agg_ref[x, y:y + 1, :] == levels, row, 0.0)
    to_x = [to_side(0), to_side(1)]
    sib_copy.wait_recv()
    parts = jnp.concatenate([total + sib_in[...]] + to_x + [jnp.where(core == 0, down, up)], axis=0)
    high = parts.astype(bf16)
    middle, low = halves(parts - high.astype(f32))
    sums = lax.dot_general(
        jnp.ones((16, 3 * EZ), bf16), jnp.concatenate([high, middle, low], axis=1),
        (((1,), (1,)), ((), ())), preferred_element_type=f32)
    direct_first(sums[0:1])
    for s in (0, 1):
        start(face1, s, SIDE - 1)

    for c in range(SIDE):
        for s in (2, 3):
            arrive1(s, c)
    gather_second(r1a, s2a, r2a, gsem_a)

    def side_y(i, carry):
        second(i + 1, 0)
        second(i + 1, SIDE - 1)
        second_own(i + 1, 0)
        second_own(i + 1, SIDE - 1)
        return carry

    lax.fori_loop(0, 2, side_y, 0)
    for c in (1, 2):
        for s in (2, 3):
            start(face2, s, c)

    for c in range(SIDE):
        arrive1(0, c)
        arrive1(1, c)
        second(0, c)
        second(SIDE - 1, c)
        start(face2, 0, c)
        start(face2, 1, c)
        if c in (0, SIDE - 1):
            s = 3 if c == 0 else 2
            start(face2, s, 0)
            start(face2, s, SIDE - 1)
        second_own(0, c)
        second_own(SIDE - 1, c)


    def last(x, y):
        col, slot = x * SIDE + y, (x + 1) * PADS + y + 1
        base_ref[col] += side_part(p2h, p2l, slot)

    def last_interior(i, carry):
        last(1, i + 1)
        last(2, i + 1)
        return carry

    lax.fori_loop(0, 2, last_interior, 0)

    for c in range(SIDE):
        for s in (2, 3):
            arrive2(s, c)

    def last_y(i, carry):
        last(i + 1, 0)
        last(i + 1, SIDE - 1)
        return carry

    lax.fori_loop(0, 2, last_y, 0)

    gains = [jnp.sum(m * p_row, axis=1, keepdims=True) for m in scaled]
    own_gain = p_col - jnp.sum(own_scaled * p_row, axis=1, keepdims=True)
    lane = iota((NP, 256), 1)
    at = lane % 64

    def coefficients(col, carry):
        x, y = col // SIDE, col % SIDE
        places = (
            jnp.where(x > 0, col - SIDE, COLS + y),
            jnp.where(x < SIDE - 1, col + SIDE, COLS + SIDE + y),
            jnp.where(y > 0, col - 1, COLS + 2 * SIDE + x),
            jnp.where(y < SIDE - 1, col + 1, COLS + 3 * SIDE + x),
            2 * COLS + col,
            3 * COLS + col,
        )
        matrix = jnp.where(at == col, own_gain, 0.0)
        for d in range(6):
            matrix = jnp.where(at == places[d], gains[d], matrix)
        high, low = halves(matrix)
        coef_ref[col] = jnp.where(lane < 128, high.astype(f32), low.astype(f32)).astype(bf16)
        return carry

    lax.fori_loop(0, COLS, coefficients, 0)
    direct_second()

    for c in range(SIDE):
        arrive2(0, c)
        arrive2(1, c)
        last(0, c)
        last(SIDE - 1, c)

    gather_third(r1a, r2a, gsem_a, gpiv_ref)
    direct_third(grhs_ref)

    for s in range(4):
        @pl.when(sends[s])
        def _(s=s):
            labels(s).wait_send()
            paths(s).wait_send()
            for c in range(SIDE):
                face1(s, c).wait_send()
                face2(s, c).wait_send()


def finish_kernel(
    gxn, gyn, zn,
    base_ref, coef_ref, grhs_ref, gpiv_ref, labels,
    out_hbm, corr_ref,
    out_v, coarse, lifted, out_sem,
):
    gx, gy = lax.axis_index("gx"), lax.axis_index("gy")
    lane, sub = iota((8, 128), 1), iota((8, 128), 0)
    level = lane % KC

    rhs = [grhs_ref[i] for i in range(zn)]
    pivot = [gpiv_ref[i] for i in range(zn)]

    def sweep(now):
        new = []
        wrap_low = jnp.where(lane < KC, 0.0, pltpu.roll(now[zn - 1], KC, 1))
        wrap_high = jnp.where(lane >= 128 - KC, 0.0, pltpu.roll(now[0], 128 - KC, 1))
        for i in range(zn):
            value = now[i]
            total = rhs[i] + (now[i - 1] if i > 0 else wrap_low)
            total += now[i + 1] if i < zn - 1 else wrap_high
            total += jnp.where(sub == 0, 0.0, pltpu.roll(value, 1, 0))
            total += jnp.where(sub == 7, 0.0, pltpu.roll(value, 7, 0))
            total += jnp.where(level == 0, 0.0, pltpu.roll(value, 1, 1))
            total += jnp.where(level == KC - 1, 0.0, pltpu.roll(value, 127, 1))
            new.append(total * pivot[i])
        return tuple(new)

    now = tuple(a * b for a, b in zip(rhs, pivot))
    for repeat in range(ITC - 1):
        now = sweep(now)
    for i in range(zn):
        coarse[i] = now[i]

    def table(ax, ay):
        shifted = ax + zn
        value = coarse[shifted % zn]
        value = jnp.where((sub == ay) & (lane // KC == shifted // zn - 1), value, 0.0)
        row = jnp.sum(value, axis=0, keepdims=True)
        row = row + pltpu.roll(row, 64, 1)
        return row + pltpu.roll(row, 32, 1)

    own = table(gx, gy)
    corr_ref[0] = own[:, :KC]
    sides = [table(gx - 1, gy), table(gx + 1, gy), table(gx, gy - 1), table(gx, gy + 1)]
    tables = [jnp.broadcast_to(own, (8, 128))] * 2 + [
        jnp.where(sub < 4, sides[0], sides[1]), jnp.where(sub < 4, sides[2], sides[3])]
    for i in range(4):
        for half in range(2):
            picked = labels[i * 8:i * 8 + 8, half * 128:half * 128 + 128].astype(jnp.int32)
            lifted[i * 8:i * 8 + 8, half * 128:half * 128 + 128] = jnp.take_along_axis(
                tables[i], picked, axis=1)
    lifted[32:48, :] = after(lifted[0:16, :])
    lifted[48:64, :] = before(lifted[0:16, :])
    high, low = halves(lifted[...])
    around = jnp.concatenate([high, low, high, low], axis=0)

    def store(x):
        return pltpu.make_async_copy(
            out_v.at[pl.ds(x * SIDE, SIDE)], out_hbm.at[x], out_sem.at[x])

    for x in range(SIDE):
        for y in range(SIDE):
            col = x * SIDE + y
            out_v[col] = base_ref[col] + jnp.dot(coef_ref[col], around, preferred_element_type=f32)
        store(x).start()
    for x in range(SIDE):
        store(x).wait()


def body(gxn, gyn, zn, right_side, diffusivity, agglomerate, element_matrix, face_matrices,
         restriction, prolongation, coarse_shift):
    group = gxn // zn * gyn
    vmem = pl.BlockSpec(memory_space=pltpu.VMEM)
    hbm = pl.BlockSpec(memory_space=pl.ANY)
    dma = pltpu.SemaphoreType.DMA
    field = pltpu.VMEM((COLS, NP, EZ), f32)
    halo = pltpu.VMEM((4, SIDE, NP, EZ), f32)
    parts = pltpu.VMEM((PADS * PADS, NP, EZ), bf16)
    gather = [
        pltpu.VMEM((1, 128), f32),
        pltpu.VMEM((group, 1, 128), f32),
        pltpu.VMEM((8, 128), f32),
        pltpu.VMEM((zn, 8, 128), f32),
    ]
    direct = [
        pltpu.VMEM((1, 128), f32),
        pltpu.VMEM((gxn * gyn // 2, 1, 128), f32),
        pltpu.VMEM((zn, 8, 128), f32),
        pltpu.VMEM((zn, 8, 128), f32),
    ]
    side_groups = pltpu.VMEM((4, SIDE, 8, EZ), f32)
    side_rows = pltpu.VMEM((4, 2 * SIDE, EZ), f32)
    placed = pltpu.VMEM((gxn // zn, zn, 8, 128), f32)
    sibling = pltpu.VMEM((KC, EZ), f32)
    base, coef, grhs, gpiv, labels = pl.pallas_call(
        functools.partial(exchange_kernel, gxn, gyn, zn),
        out_shape=(
            jax.ShapeDtypeStruct((COLS, NP, EZ), f32),
            jax.ShapeDtypeStruct((COLS, NP, 256), bf16),
            jax.ShapeDtypeStruct((zn, 8, 128), f32),
            jax.ShapeDtypeStruct((zn, 8, 128), f32),
            jax.ShapeDtypeStruct((2 * COLS, EZ), f32),
        ),
        in_specs=[pl.BlockSpec(memory_space=pltpu.HBM)] * 8,
        out_specs=(vmem,) * 5,
        scratch_shapes=[
            pltpu.VMEM((SIDE, SIDE, EZ), f32), pltpu.VMEM((SIDE, SIDE, EZ), jnp.int32),
            pltpu.VMEM((NP, NP), f32), pltpu.VMEM((6, NP, NP), f32), pltpu.VMEM((NP,), f32),
            pltpu.VMEM((NP,), f32), pltpu.VMEM((1, 1, KC), f32),
            field, field, field, halo, halo, parts, parts, parts, parts,
            pltpu.VMEM((192, 256), bf16), pltpu.VMEM((128, 256), bf16), pltpu.VMEM((64, 256), bf16),
            field, side_groups, side_groups,
            pltpu.VMEM((COLS, 8, EZ), f32), side_rows, side_rows, placed, sibling, sibling,
            *gather, *direct,
            dma((7,)), dma((SIDE,)), dma((4, SIDE)), dma((4, SIDE)), dma((4, SIDE)), dma((4, SIDE)),
            *[dma((4,))] * 6, dma((2,)), pltpu.SemaphoreType.REGULAR,
        ],
        compiler_params=pltpu.CompilerParams(
            collective_id=0, has_side_effects=True, vmem_limit_bytes=40 * 2**20),
        name="exchange",
    )(*[pltpu.with_memory_space_constraint(value, pltpu.HBM) for value in (
        right_side, diffusivity, agglomerate, element_matrix, face_matrices, restriction,
        prolongation, coarse_shift)])
    return pl.pallas_call(
        functools.partial(finish_kernel, gxn, gyn, zn),
        out_shape=(
            jax.ShapeDtypeStruct((SIDE, SIDE, NP, EZ), f32),
            jax.ShapeDtypeStruct((1, 1, KC), f32),
        ),
        in_specs=[vmem] * 5,
        out_specs=(hbm, vmem),
        scratch_shapes=[
            field, pltpu.VMEM((zn, 8, 128), f32), pltpu.VMEM((64, EZ), f32), dma((SIDE,)),
        ],
        compiler_params=pltpu.CompilerParams(vmem_limit_bytes=20 * 2**20),
        name="finish",
    )(base, coef, grhs, gpiv, labels)


def solution(mesh):
    gxn, gyn = mesh.shape["gx"], mesh.shape["gy"]
    return jax.shard_map(
        functools.partial(body, gxn, gyn, max(1, gxn // 4)),
        mesh=mesh,
        in_specs=(
            P("gx", "gy", None, None),
            P("gx", "gy", None),
            P("gx", "gy", None),
            P(),
            P(),
            P(),
            P(),
            P("gx", "gy", None),
        ),
        out_specs=(P("gx", "gy", None, None), P("gx", "gy", None)),
        check_vma=False,
    )
```

```python
import functools

import jax
import jax.numpy as jnp
from jax import lax
from jax.experimental import pallas as pl
from jax.experimental.pallas import tpu as pltpu
from jax.sharding import PartitionSpec as P

NP = 64
EZ = 256
KC = 32
ITC = 24
SIDE = 4
COLS = SIDE * SIDE
PADS = SIDE + 2
damping = 0.8
SPLIT = 3
highest = lax.Precision.HIGHEST
MESH = pl.DeviceIdType.MESH
f32, bf16 = jnp.float32, jnp.bfloat16


def halves(values):
    high = values.astype(bf16)
    return high, (values - high.astype(f32)).astype(bf16)


def iota(shape, axis):
    return lax.broadcasted_iota(jnp.int32, shape, axis)


def after(rows):
    return jnp.where(iota(rows.shape, 1) == 0, 0.0, pltpu.roll(rows, 1, 1))


def before(rows):
    last = rows.shape[1] - 1
    return jnp.where(iota(rows.shape, 1) == last, 0.0, pltpu.roll(rows, last, 1))


SOURCE = (
    lambda c: (SIDE - 1) * SIDE + c,
    lambda c: c,
    lambda c: c * SIDE + SIDE - 1,
    lambda c: c * SIDE,
)


def padded_slot(side, c):
    return (c + 1, (PADS - 1) * PADS + c + 1, (c + 1) * PADS, (c + 1) * PADS + PADS - 1)[side]


def exchange_kernel(
    gxn, gyn, zn,
    rhs_hbm, w_hbm, agg_hbm, e_hbm, f_hbm, r_hbm, p_hbm, shift_hbm,
    base_ref, coef_ref, coarse_ref, labels_ref,
    w_ref, agg_ref, e_ref, f_ref, r_ref, p_ref, shift_ref, rhs_v, u1, u2, hal1, hal2, p1h, p1l, p2h, p2l, own_w, side_w, path_w,
    field, qsend, qhalo, trow, asend, ahalo, placed, sib_out, sib_in,
    s1a, r1a, s2a, r2a, s1b, r1b, s2b, r2b,
    small_sem, load_sem, send1, recv1, send2, recv2, asend_sem, arecv_sem,
    gsem_a, gsem_b, qsend_sem, qrecv_sem, sib_sem, all_in,
):
    gx, gy = lax.axis_index("gx"), lax.axis_index("gy")
    xg, zg = gx // zn, gx % zn
    xn = gxn // zn
    group = xn * gyn
    mine = xg * gyn + gy
    has = (gx > 0, gx < gxn - 1, gy > 0, gy < gyn - 1)
    sends = (has[1], has[0], has[3], has[2])
    target = ((gx + 1, gy), (gx - 1, gy), (gx, gy + 1), (gx, gy - 1))

    def load(x):
        return pltpu.make_async_copy(
            rhs_hbm.at[x], rhs_v.at[pl.ds(x * SIDE, SIDE)], load_sem.at[x])

    inputs = [
        pltpu.make_async_copy(a, b, small_sem.at[i]) for i, (a, b) in enumerate((
            (e_hbm, e_ref), (f_hbm, f_ref), (r_hbm, r_ref), (p_hbm, p_ref), (w_hbm, w_ref),
            (shift_hbm, shift_ref), (agg_hbm, agg_ref)))]
    for copy in inputs:
        copy.start()
    for x in (0, 3, 1, 2):
        load(x).start()

    barrier = pltpu.get_barrier_semaphore()
    for s in (0, 1):
        @pl.when(sends[s])
        def _(s=s):
            pl.semaphore_signal(barrier, inc=1, device_id=target[s], device_id_type=MESH)

    def greet_plane(j, carry):
        @pl.when(j != mine)
        def _():
            pl.semaphore_signal(
                barrier, inc=1, device_id=((j // gyn) * zn + zg, j % gyn), device_id_type=MESH)
        return carry

    lax.fori_loop(0, group, greet_plane, 0)

    def greet_line(j, carry):
        @pl.when(j != zg)
        def _():
            pl.semaphore_signal(
                barrier, inc=1, device_id=(xg * zn + j, gy), device_id_type=MESH)
        return carry

    lax.fori_loop(0, zn, greet_line, 0)

    for copy in inputs:
        copy.wait()

    same = iota((NP, NP), 0) == iota((NP, NP), 1)
    element = e_ref[...]
    on_diagonal = jnp.where(same, element, 0.0)
    diagonal = jnp.sum(on_diagonal, axis=1, keepdims=True)
    scale = damping / diagonal
    r_row = r_ref[...].reshape(1, NP)
    p_row = p_ref[...].reshape(1, NP)
    r_col = jnp.sum(jnp.where(same, r_row, 0.0), axis=1, keepdims=True)
    p_col = jnp.sum(jnp.where(same, p_row, 0.0), axis=1, keepdims=True)
    faces = [f_ref[d] for d in range(6)]
    scaled = [scale * face for face in faces]
    own_scaled = scale * element
    rows = [jnp.sum(r_col * m, axis=0, keepdims=True) for m in [element] + faces]
    rows.append(r_row * jnp.sum(on_diagonal, axis=0, keepdims=True) / damping)

    def lay(weights, matrix):
        high, low = halves(matrix)
        weights[:, 0:64] = high
        weights[:, 64:128] = high
        weights[:, 128:192] = low
        weights[:, 192:256] = low

    lay(own_w, jnp.concatenate([own_scaled, scaled[4], scaled[5]], axis=0))

    reduce_rows = jnp.concatenate(rows[0:7] + [jnp.zeros((1, NP), f32)], axis=0)
    scaled_rows = reduce_rows * (damping / jnp.sum(on_diagonal, axis=0, keepdims=True))
    products = [jnp.dot(scaled_rows, m, precision=highest, preferred_element_type=f32)
                for m in [element] + faces]
    lay(path_w, jnp.concatenate(
        [2.0 * reduce_rows - products[0]] + products[1:] + [rows[7], jnp.zeros((7, NP), f32)], axis=0))
    for d in range(4):
        high, low = halves(scaled[d])
        side_w[0:64, d * 64:d * 64 + 64] = high
        side_w[64:128, d * 64:d * 64 + 64] = low

    for x in (0, 3, 1, 2):
        load(x).wait()

        def first(y, carry, x=x):
            col = x * SIDE + y
            value = rhs_v[col] * (1.0 / w_ref[x, pl.ds(y, 1), :]) * scale
            u1[col] = value
            slot = (x + 1) * PADS + y + 1
            p1h[slot], p1l[slot] = halves(value)
            return carry

        lax.fori_loop(0, SIDE, first, 0)

    for x in range(SIDE):
        labels_ref[x * SIDE:(x + 1) * SIDE, :] = agg_ref[x].astype(f32)
    for s in range(4):
        for c in range(SIDE):
            x, y = SOURCE[s](c) // SIDE, SOURCE[s](c) % SIDE
            asend[s, c:c + 1, :] = w_ref[x, y:y + 1, :]
            asend[s, SIDE + c:SIDE + c + 1, :] = agg_ref[x, y:y + 1, :].astype(f32)
    placed[...] = jnp.zeros_like(placed)

    in_group = iota((1, 128), 1) // KC == xg

    def spread(row):
        return jnp.where(in_group, jnp.concatenate([row] * 4, axis=1), 0.0)

    def follow(x, carry):
        for y in range(SIDE):
            col, slot = x * SIDE + y, (x + 1) * PADS + y + 1
            high, low = p1h[slot], p1l[slot]
            field[col] = jnp.dot(path_w[...], jnp.concatenate([high, low, high, low], axis=0),
                                 preferred_element_type=f32)
        return carry

    lax.fori_loop(0, SIDE, follow, 0)
    for s in range(4):
        for c in range(SIDE):
            qsend[s, c] = field[SOURCE[s](c), 8 + 8 * s:16 + 8 * s, :]

    expected = group - 1 + zn - 1 + has[0].astype(jnp.int32) + has[1].astype(jnp.int32)
    pl.semaphore_wait(barrier, expected)

    def face(values, halo, send, recv, s, c):
        return pltpu.make_async_remote_copy(
            src_ref=values.at[SOURCE[s](c)], dst_ref=halo.at[s, c],
            send_sem=send.at[s, c], recv_sem=recv.at[s, c],
            device_id=target[s], device_id_type=MESH)

    face1 = functools.partial(face, u1, hal1, send1, recv1)
    face2 = functools.partial(face, u2, hal2, send2, recv2)

    def start(make, s, c):
        @pl.when(sends[s])
        def _():
            make(s, c).start()

    def small(values, halo, send, recv, s):
        return pltpu.make_async_remote_copy(
            src_ref=values.at[s], dst_ref=halo.at[s], send_sem=send.at[s], recv_sem=recv.at[s],
            device_id=target[s], device_id_type=MESH)

    paths = functools.partial(small, qsend, qhalo, qsend_sem, qrecv_sem)
    labels = functools.partial(small, asend, ahalo, asend_sem, arecv_sem)

    for s in range(4):
        @pl.when(sends[s])
        def _(s=s):
            paths(s).start()
            labels(s).start()
    for c in range(SIDE):
        for s in (0, 1, 2, 3) if c < SIDE - 1 else (2, 3):
            start(face1, s, c)

    def gather_first(s1, r1, sems, row):
        s1[...] = row
        r1[mine] = row

        def step(j, carry):
            @pl.when(j != mine)
            def _():
                pltpu.make_async_remote_copy(
                    src_ref=s1, dst_ref=r1.at[mine], send_sem=sems.at[0], recv_sem=sems.at[1],
                    device_id=((j // gyn) * zn + zg, j % gyn), device_id_type=MESH).start()
            return carry

        lax.fori_loop(0, group, step, 0)

    def wait_bytes(ref, count, sem):
        part = ref.at[pl.ds(0, count)]
        pltpu.make_async_copy(part, part, sem).wait()

    def gather_second(r1, s2, r2, sems):
        wait_bytes(r1, group - 1, sems.at[1])
        if gyn < 8:
            s2[...] = jnp.zeros_like(s2)
        for b in range(gyn):
            s2[b:b + 1, :] = sum(r1[q * gyn + b] for q in range(xn))
        r2[zg] = s2[...]

        def step(j, carry):
            @pl.when(j != zg)
            def _():
                pltpu.make_async_remote_copy(
                    src_ref=s2, dst_ref=r2.at[zg], send_sem=sems.at[2], recv_sem=sems.at[3],
                    device_id=(xg * zn + j, gy), device_id_type=MESH).start()
            return carry

        lax.fori_loop(0, zn, step, 0)

    def pass_on(j, carry):
        @pl.when(j != zg)
        def _():
            pl.semaphore_signal(
                all_in, inc=1, device_id=(xg * zn + j, gy), device_id_type=MESH)
        return carry

    lax.fori_loop(0, zn, pass_on, 0)
    core, yg, yn = gy % 2, gy // 2, gyn // 2
    chips = gxn * yn

    def far_first(size):
        half = size // 2
        return [half - (k + 1) // 2 if k % 2 else half + k // 2 for k in range(size)]

    def direct_first(rows):
        s1b[...] = rows
        r1b[gx * yn + yg] = rows
        pl.semaphore_wait(all_in, zn - 1)

        def send(dx, dy, to_z):
            to_x = (xg + dx) % xn * zn + to_z
            pltpu.make_async_remote_copy(
                src_ref=s1b, dst_ref=r1b.at[gx * yn + yg], send_sem=gsem_b.at[0],
                recv_sem=gsem_b.at[1],
                device_id=(to_x, (yg + dy) % yn * 2 + core), device_id_type=MESH).start()

        offsets = [(dx, dy) for dx in far_first(xn) for dy in far_first(yn)]

        def step(k, carry):
            to_z = (zg + jnp.where(k % 2 == 1, zn // 2 - (k + 1) // 2, zn // 2 + k // 2)) % zn
            for dx, dy in offsets:
                send(dx, dy, to_z)
            return carry

        lax.fori_loop(0, zn - 1, step, 0)
        for dx, dy in offsets[:-1]:
            send(dx, dy, zg)

    pair = pltpu.make_async_remote_copy(
        src_ref=s2b, dst_ref=r2b, send_sem=gsem_b.at[2], recv_sem=gsem_b.at[3],
        device_id=(gx, gy + 1 - 2 * core), device_id_type=MESH)

    def direct_second():
        wait_bytes(r1b, chips - 1, gsem_b.at[1])
        for q in range(xn):
            for i in range(zn):
                for y in range(yn):
                    at = (q * zn + i) * yn + y
                    placed[q, i, pl.ds(2 * y + core, 1), :] = r1b[at]
        kind, sub = iota((8, 128), 1) // KC, iota((8, 128), 0)
        zero = jnp.zeros((8, 128), f32)
        step_y, edge = jnp.where(core == 1, 1, 7), jnp.where(core == 1, 0, 7)

        def source(q, i):
            return placed[q, i] if q < xn else zero

        for i in range(zn):
            total = zero
            for r in range(4):
                own = source(r, i)
                if i > 0:
                    left = source((1 + r) % 4, i - 1)
                else:
                    left = source(r, zn - 1) if r < 3 else zero
                if i < zn - 1:
                    right = source((2 + r) % 4, i + 1)
                else:
                    right = source((3 + r) % 4, 0) if (3 + r) % 4 else zero
                beside = jnp.where(
                    sub == edge, 0.0, pltpu.roll(source((3 + r) % 4, i), step_y, 0))
                moved = jnp.where(kind < 2, jnp.where(kind == 0, own, left),
                                  jnp.where(kind == 2, right, beside))
                total += pltpu.roll(moved, KC * r, 1) if r else moved
            s2b[i] = total
        pair.start()

    def solve_coarse():
        wait_bytes(r2a, zn - 1, gsem_a.at[3])
        pair.wait_recv()
        now = coarse_sweeps([s2b[i] + r2b[i] for i in range(zn)], [r2a[i] for i in range(zn)])
        for i in range(zn):
            coarse_ref[i] = now[i]

    gather_first(s1a, r1a, gsem_a, spread(1.0 / (6.0 + shift_ref[0])))

    nothing = jnp.zeros((NP, EZ), bf16)
    for s in range(4):
        @pl.when(jnp.logical_not(has[s]))
        def _(s=s):
            qhalo[s] = jnp.zeros((SIDE, 8, EZ), f32)
            ahalo[s] = jnp.zeros((2 * SIDE, EZ), f32)
            for c in range(SIDE):
                slot = padded_slot(s, c)
                p1h[slot] = nothing
                p1l[slot] = nothing
                p2h[slot] = nothing
                p2l[slot] = nothing

    own_matrix = own_w
    side_matrix = side_w

    def own_part(high_ref, low_ref, slot):
        high, low = high_ref[slot], low_ref[slot]
        g = jnp.dot(own_matrix[...], jnp.concatenate([high, low, high, low], axis=0),
                    preferred_element_type=f32)
        return g[0:64] - after(g[64:128]) - before(g[128:192])

    def side_part(high_ref, low_ref, slot):
        around = (slot - PADS, slot + PADS, slot - 1, slot + 1)
        high = jnp.concatenate([high_ref[s] for s in around], axis=0)
        low = jnp.concatenate([low_ref[s] for s in around], axis=0)
        both = jnp.dot(side_matrix[...], high, preferred_element_type=f32)
        return both[0:64] + both[64:128] + jnp.dot(
            side_matrix[0:64, :], low, preferred_element_type=f32)

    def second(x, y):
        col, slot = x * SIDE + y, (x + 1) * PADS + y + 1
        before_it = u1[col]
        value = 2.0 * before_it - own_part(p1h, p1l, slot) + side_part(p1h, p1l, slot)
        u2[col] = value
        p2h[slot], p2l[slot] = halves(value)

    def second_own(x, y):
        col, slot = x * SIDE + y, (x + 1) * PADS + y + 1
        base_ref[col] = u2[col] + u1[col] - own_part(p2h, p2l, slot)

    def arrive(make, halo, high_ref, low_ref, s, c):
        @pl.when(has[s])
        def _():
            make(s, c).wait_recv()
            slot = padded_slot(s, c)
            high_ref[slot], low_ref[slot] = halves(halo[s, c])

    arrive1 = functools.partial(arrive, face1, hal1, p1h, p1l)
    arrive2 = functools.partial(arrive, face2, hal2, p2h, p2l)

    def interior(i, carry):
        second(1, i + 1)
        second(2, i + 1)
        second_own(1, i + 1)
        second_own(2, i + 1)
        return carry

    lax.fori_loop(0, 2, interior, 0)

    for s in range(4):
        @pl.when(has[s])
        def _(s=s):
            paths(s).wait_recv()
            labels(s).wait_recv()
    for x in range(SIDE):
        for y in range(SIDE):
            col = x * SIDE + y
            value = field[col, 0:8, :] + after(field[col, 40:48, :]) + before(field[col, 48:56, :])
            value += field[col - SIDE, 8:16, :] if x > 0 else qhalo[0, y]
            value += field[col + SIDE, 16:24, :] if x < SIDE - 1 else qhalo[1, y]
            value += field[col - 1, 24:32, :] if y > 0 else qhalo[2, x]
            value += field[col + 1, 32:40, :] if y < SIDE - 1 else qhalo[3, x]
            total = field[col, 56:57, :] - value[0:1] + after(value[5:6]) + before(value[6:7])
            trow[col] = jnp.where(iota((8, EZ), 0) == 0, total, value)

    for s in range(4):
        labels_ref[COLS + s * SIDE:COLS + (s + 1) * SIDE, :] = ahalo[s, SIDE:2 * SIDE, :]
    levels = iota((KC, EZ), 0)
    float_levels = levels.astype(f32)

    def to_side(s):
        total = jnp.zeros((KC, EZ), f32)
        side = s + 1 - 2 * (s % 2)
        for c in range(SIDE):
            row = trow[SOURCE[s](c), s + 1:s + 2, :] * ahalo[side, c:c + 1, :]
            total += jnp.where(ahalo[side, SIDE + c:SIDE + c + 1, :] == float_levels, row, 0.0)
        return total

    up, down = to_side(2), to_side(3)
    sib_out[...] = jnp.where(core == 0, up, down)
    sib_copy = pltpu.make_async_remote_copy(
        src_ref=sib_out, dst_ref=sib_in, send_sem=sib_sem.at[0], recv_sem=sib_sem.at[1],
        device_id=(gx, gy + 1 - 2 * core), device_id_type=MESH)
    sib_copy.start()
    total = jnp.zeros((KC, EZ), f32)
    for x in range(SIDE):
        for y in range(SIDE):
            col = x * SIDE + y
            row = trow[col, 0:1, :]
            if x > 0:
                row += trow[col - SIDE, 1:2, :]
            if x < SIDE - 1:
                row += trow[col + SIDE, 2:3, :]
            if y > 0:
                row += trow[col - 1, 3:4, :]
            if y < SIDE - 1:
                row += trow[col + 1, 4:5, :]
            row = row * w_ref[x, y:y + 1, :]
            total += jnp.where(agg_ref[x, y:y + 1, :] == levels, row, 0.0)
    to_x = [to_side(0), to_side(1)]
    sib_copy.wait_recv()
    parts = jnp.concatenate([total + sib_in[...]] + to_x + [jnp.where(core == 0, down, up)], axis=0)
    high = parts.astype(bf16)
    middle, low = halves(parts - high.astype(f32))
    sums = lax.dot_general(
        jnp.ones((16, 3 * EZ), bf16), jnp.concatenate([high, middle, low], axis=1),
        (((1,), (1,)), ((), ())), preferred_element_type=f32)
    direct_first(sums[0:1])
    for s in (0, 1):
        start(face1, s, SIDE - 1)

    for c in range(SIDE):
        for s in (2, 3):
            arrive1(s, c)
    gather_second(r1a, s2a, r2a, gsem_a)

    def side_y(i, carry):
        second(i + 1, 0)
        second(i + 1, SIDE - 1)
        second_own(i + 1, 0)
        second_own(i + 1, SIDE - 1)
        return carry

    lax.fori_loop(0, 2, side_y, 0)
    for c in (1, 2):
        for s in (2, 3):
            start(face2, s, c)

    for c in range(SIDE):
        arrive1(0, c)
        arrive1(1, c)
        second(0, c)
        second(SIDE - 1, c)
        start(face2, 0, c)
        start(face2, 1, c)
        if c in (0, SIDE - 1):
            s = 3 if c == 0 else 2
            start(face2, s, 0)
            start(face2, s, SIDE - 1)
        second_own(0, c)
        second_own(SIDE - 1, c)


    def last(x, y):
        col, slot = x * SIDE + y, (x + 1) * PADS + y + 1
        base_ref[col] += side_part(p2h, p2l, slot)

    def last_interior(i, carry):
        last(1, i + 1)
        last(2, i + 1)
        return carry

    lax.fori_loop(0, 2, last_interior, 0)

    for c in range(SIDE):
        for s in (2, 3):
            arrive2(s, c)

    def last_y(i, carry):
        last(i + 1, 0)
        last(i + 1, SIDE - 1)
        return carry

    lax.fori_loop(0, 2, last_y, 0)

    gains = [jnp.sum(m * p_row, axis=1, keepdims=True) for m in scaled]
    own_gain = p_col - jnp.sum(own_scaled * p_row, axis=1, keepdims=True)
    lane = iota((NP, 256), 1)
    at = lane % 64

    def coefficients(col, carry):
        x, y = col // SIDE, col % SIDE
        places = (
            jnp.where(x > 0, col - SIDE, COLS + y),
            jnp.where(x < SIDE - 1, col + SIDE, COLS + SIDE + y),
            jnp.where(y > 0, col - 1, COLS + 2 * SIDE + x),
            jnp.where(y < SIDE - 1, col + 1, COLS + 3 * SIDE + x),
            2 * COLS + col,
            3 * COLS + col,
        )
        matrix = jnp.where(at == col, own_gain, 0.0)
        for d in range(6):
            matrix = jnp.where(at == places[d], gains[d], matrix)
        high, low = halves(matrix)
        coef_ref[col] = jnp.where(lane < 128, high.astype(f32), low.astype(f32)).astype(bf16)
        return carry

    lax.fori_loop(0, COLS, coefficients, 0)
    direct_second()

    for c in range(SIDE):
        if c == SPLIT:
            solve_coarse()
        arrive2(0, c)
        arrive2(1, c)
        last(0, c)
        last(SIDE - 1, c)

    wait_bytes(r1a, group - 1, gsem_a.at[0])
    wait_bytes(r2a, zn - 1, gsem_a.at[2])
    wait_bytes(r1b, chips - 1, gsem_b.at[0])
    pair.wait_send()
    sib_copy.wait_send()

    for s in range(4):
        @pl.when(sends[s])
        def _(s=s):
            labels(s).wait_send()
            paths(s).wait_send()
            for c in range(SIDE):
                face1(s, c).wait_send()
                face2(s, c).wait_send()


def coarse_sweeps(rhs, pivot):
    zn = len(rhs)
    lane, sub = iota((8, 128), 1), iota((8, 128), 0)
    level = lane % KC

    def sweep(repeat, now):
        new = []
        wrap_low = jnp.where(lane < KC, 0.0, pltpu.roll(now[zn - 1], KC, 1))
        wrap_high = jnp.where(lane >= 128 - KC, 0.0, pltpu.roll(now[0], 128 - KC, 1))
        for i in range(zn):
            value = now[i]
            total = rhs[i] + (now[i - 1] if i > 0 else wrap_low)
            total += now[i + 1] if i < zn - 1 else wrap_high
            total += jnp.where(sub == 0, 0.0, pltpu.roll(value, 1, 0))
            total += jnp.where(sub == 7, 0.0, pltpu.roll(value, 7, 0))
            total += jnp.where(level == 0, 0.0, pltpu.roll(value, 1, 1))
            total += jnp.where(level == KC - 1, 0.0, pltpu.roll(value, 127, 1))
            new.append(total * pivot[i])
        return tuple(new)

    return lax.fori_loop(0, ITC - 1, sweep, tuple(a * b for a, b in zip(rhs, pivot)))


def finish_kernel(
    gxn, gyn, zn,
    base_ref, coef_ref, coarse, labels,
    out_hbm, corr_ref,
    out_v, lifted, out_sem,
):
    gx, gy = lax.axis_index("gx"), lax.axis_index("gy")
    lane, sub = iota((8, 128), 1), iota((8, 128), 0)

    def table(ax, ay):
        shifted = ax + zn
        value = coarse[shifted % zn]
        value = jnp.where((sub == ay) & (lane // KC == shifted // zn - 1), value, 0.0)
        row = jnp.sum(value, axis=0, keepdims=True)
        row = row + pltpu.roll(row, 64, 1)
        return row + pltpu.roll(row, 32, 1)

    own = table(gx, gy)
    corr_ref[0] = own[:, :KC]
    sides = [table(gx - 1, gy), table(gx + 1, gy), table(gx, gy - 1), table(gx, gy + 1)]
    tables = [jnp.broadcast_to(own, (8, 128))] * 2 + [
        jnp.where(sub < 4, sides[0], sides[1]), jnp.where(sub < 4, sides[2], sides[3])]
    for i in range(4):
        for half in range(2):
            picked = labels[i * 8:i * 8 + 8, half * 128:half * 128 + 128].astype(jnp.int32)
            lifted[i * 8:i * 8 + 8, half * 128:half * 128 + 128] = jnp.take_along_axis(
                tables[i], picked, axis=1)
    lifted[32:48, :] = after(lifted[0:16, :])
    lifted[48:64, :] = before(lifted[0:16, :])
    high, low = halves(lifted[...])
    around = jnp.concatenate([high, low, high, low], axis=0)

    def store(x):
        return pltpu.make_async_copy(
            out_v.at[pl.ds(x * SIDE, SIDE)], out_hbm.at[x], out_sem.at[x])

    for x in range(SIDE):
        for y in range(SIDE):
            col = x * SIDE + y
            out_v[col] = base_ref[col] + jnp.dot(coef_ref[col], around, preferred_element_type=f32)
        store(x).start()
    for x in range(SIDE):
        store(x).wait()


def body(gxn, gyn, zn, right_side, diffusivity, agglomerate, element_matrix, face_matrices,
         restriction, prolongation, coarse_shift):
    group = gxn // zn * gyn
    vmem = pl.BlockSpec(memory_space=pltpu.VMEM)
    hbm = pl.BlockSpec(memory_space=pl.ANY)
    dma = pltpu.SemaphoreType.DMA
    field = pltpu.VMEM((COLS, NP, EZ), f32)
    halo = pltpu.VMEM((4, SIDE, NP, EZ), f32)
    parts = pltpu.VMEM((PADS * PADS, NP, EZ), bf16)
    gather = [
        pltpu.VMEM((1, 128), f32),
        pltpu.VMEM((group, 1, 128), f32),
        pltpu.VMEM((8, 128), f32),
        pltpu.VMEM((zn, 8, 128), f32),
    ]
    direct = [
        pltpu.VMEM((1, 128), f32),
        pltpu.VMEM((gxn * gyn // 2, 1, 128), f32),
        pltpu.VMEM((zn, 8, 128), f32),
        pltpu.VMEM((zn, 8, 128), f32),
    ]
    side_groups = pltpu.VMEM((4, SIDE, 8, EZ), f32)
    side_rows = pltpu.VMEM((4, 2 * SIDE, EZ), f32)
    placed = pltpu.VMEM((gxn // zn, zn, 8, 128), f32)
    sibling = pltpu.VMEM((KC, EZ), f32)
    base, coef, coarse, labels = pl.pallas_call(
        functools.partial(exchange_kernel, gxn, gyn, zn),
        out_shape=(
            jax.ShapeDtypeStruct((COLS, NP, EZ), f32),
            jax.ShapeDtypeStruct((COLS, NP, 256), bf16),
            jax.ShapeDtypeStruct((zn, 8, 128), f32),
            jax.ShapeDtypeStruct((2 * COLS, EZ), f32),
        ),
        in_specs=[pl.BlockSpec(memory_space=pltpu.HBM)] * 8,
        out_specs=(vmem,) * 4,
        scratch_shapes=[
            pltpu.VMEM((SIDE, SIDE, EZ), f32), pltpu.VMEM((SIDE, SIDE, EZ), jnp.int32),
            pltpu.VMEM((NP, NP), f32), pltpu.VMEM((6, NP, NP), f32), pltpu.VMEM((NP,), f32),
            pltpu.VMEM((NP,), f32), pltpu.VMEM((1, 1, KC), f32),
            field, field, field, halo, halo, parts, parts, parts, parts,
            pltpu.VMEM((192, 256), bf16), pltpu.VMEM((128, 256), bf16), pltpu.VMEM((64, 256), bf16),
            field, side_groups, side_groups,
            pltpu.VMEM((COLS, 8, EZ), f32), side_rows, side_rows, placed, sibling, sibling,
            *gather, *direct,
            dma((7,)), dma((SIDE,)), dma((4, SIDE)), dma((4, SIDE)), dma((4, SIDE)), dma((4, SIDE)),
            *[dma((4,))] * 6, dma((2,)), pltpu.SemaphoreType.REGULAR,
        ],
        compiler_params=pltpu.CompilerParams(
            collective_id=0, has_side_effects=True, vmem_limit_bytes=40 * 2**20),
        name="exchange",
    )(*[pltpu.with_memory_space_constraint(value, pltpu.HBM) for value in (
        right_side, diffusivity, agglomerate, element_matrix, face_matrices, restriction,
        prolongation, coarse_shift)])
    return pl.pallas_call(
        functools.partial(finish_kernel, gxn, gyn, zn),
        out_shape=(
            jax.ShapeDtypeStruct((SIDE, SIDE, NP, EZ), f32),
            jax.ShapeDtypeStruct((1, 1, KC), f32),
        ),
        in_specs=[vmem] * 4,
        out_specs=(hbm, vmem),
        scratch_shapes=[
            field, pltpu.VMEM((64, EZ), f32), dma((SIDE,)),
        ],
        compiler_params=pltpu.CompilerParams(vmem_limit_bytes=20 * 2**20),
        name="finish",
    )(base, coef, coarse, labels)


def solution(mesh):
    gxn, gyn = mesh.shape["gx"], mesh.shape["gy"]
    return jax.shard_map(
        functools.partial(body, gxn, gyn, max(1, gxn // 4)),
        mesh=mesh,
        in_specs=(
            P("gx", "gy", None, None),
            P("gx", "gy", None),
            P("gx", "gy", None),
            P(),
            P(),
            P(),
            P(),
            P("gx", "gy", None),
        ),
        out_specs=(P("gx", "gy", None, None), P("gx", "gy", None)),
        check_vma=False,
    )
```
